512 devices in a mesh: batch: 32 (over x, y), feat: 16 (over z, core).
Axes of the slice: x: 4, y: 8, z: 8, core: 2. Of those that a mesh axis runs over, the one named last changes fastest.
Arguments:
- view_one: bfloat16 [8192, 4096], P('batch', 'feat'), may hold values from -200 to 200
- view_two: bfloat16 [8192, 4096], P('batch', 'feat'), may hold values from -200 to 200
Outputs:
- total_loss: float32 [], replicated
- grad_one: bfloat16 [8192, 4096], P('batch', 'feat')
- grad_two: bfloat16 [8192, 4096], P('batch', 'feat')
The draws below stay inside these ranges and needn't reach their ends.
All inputs are finite; a program needn't handle non-finite values.
Results may differ from the reference program's by a relative error of at most 0.017.
Values may be sent and summed in bfloat16 or wider, within the bound.
A program may use at most 64 MiB of HBM per device.

```python
import jax
import jax.numpy as jnp
from jax import lax

FEAT = 4096
B_DEV = 256
N_BATCH = 32
N_FEAT = 16


def mixed_latent(key):
    key_latent, key_order = jax.random.split(key)
    latent = jnp.clip(jax.random.normal(key_latent, (B_DEV * N_BATCH, FEAT), jnp.float32), -6.0, 6.0)
    order = jax.random.permutation(key_order, FEAT)
    return latent + 0.6 * jnp.take(latent, order, axis=1)


def assemble(shared, noise, scales, offsets, row_factor):
    value = (shared + noise) * row_factor[:, None] * scales[None, :] + offsets[None, :] * scales[None, :]
    return jnp.clip(value, -200.0, 200.0).astype(jnp.bfloat16)


def make_view(key, shared, noise_top):
    key_noise, key_scale, key_offset = jax.random.split(key, 3)
    row_total = B_DEV * N_BATCH
    block_width = FEAT // N_FEAT
    rising = 1.0 + 2.0 * jnp.arange(row_total, dtype=jnp.float32) / row_total
    place = (jnp.arange(FEAT, dtype=jnp.int32) % block_width).astype(jnp.float32) / block_width
    noise_factor = 1.0 + (noise_top - 1.0) * place
    noise = 0.15 * jnp.clip(jax.random.normal(key_noise, (row_total, FEAT), jnp.float32), -6.0, 6.0) * noise_factor[None, :]
    scales = jnp.exp(jax.random.uniform(key_scale, (FEAT,), jnp.float32, -0.69, 1.61))
    offsets = jax.random.uniform(key_offset, (FEAT,), jnp.float32, -2.0, 2.0)
    row_factor = rising
    return assemble(shared, noise, scales, offsets, row_factor)


def draw_view_one(key, part):
    shared = mixed_latent(key)
    key = jax.random.fold_in(key, 11)
    return make_view(key, shared, 1.0)


def draw_view_two(key, part):
    shared = mixed_latent(key)
    key = jax.random.fold_in(key, 12)
    return make_view(key, shared, 4.0)


def setup_inputs(seed: int = 0) -> dict:
    splits = jax.random.split(jax.random.key(seed), 3)
    return {
        "view_one": draw_view_one(jax.random.fold_in(splits[2], 71), 0),
        "view_two": draw_view_two(jax.random.fold_in(splits[2], 71), 0),
    }


OFF_WEIGHT = 0.0051
EPSILON = 1e-05
LOSS_SCALE = 16.0

def standardize(view):
    as_float = view.astype(jnp.float32)
    row_total = as_float.shape[0]
    center = lax.optimization_barrier(jnp.sum(as_float, axis=0)) / row_total
    squares = lax.optimization_barrier(jnp.sum(as_float * as_float, axis=0)) / row_total
    deviation = jnp.sqrt(squares - center * center + EPSILON)
    return (((as_float - center) / deviation).astype(jnp.bfloat16), deviation)

def reference(view_one, view_two):
    row_total = view_one.shape[0]
    norm_one, dev_one = standardize(view_one)
    norm_two, dev_two = standardize(view_two)
    cross_corr = lax.dot_general(norm_one, norm_two, (((0,), (0,)), ((), ())), preferred_element_type=jnp.float32) / row_total
    on_diagonal = jnp.eye(FEAT, dtype=bool)
    total_loss = jnp.sum(jnp.where(on_diagonal, (1.0 - cross_corr) ** 2, OFF_WEIGHT * cross_corr * cross_corr))
    grad_c = jnp.where(on_diagonal, -2.0 * (1.0 - cross_corr), 2.0 * OFF_WEIGHT * cross_corr).astype(jnp.bfloat16)
    dnorm_one = lax.dot_general(norm_two, grad_c, (((1,), (1,)), ((), ())), preferred_element_type=jnp.float32)
    dnorm_two = jnp.dot(norm_one, grad_c, preferred_element_type=jnp.float32)
    first_f = norm_one.astype(jnp.float32)
    second_f = norm_two.astype(jnp.float32)
    trace_one = lax.optimization_barrier(jnp.sum(first_f * dnorm_one, axis=0)) / row_total
    trace_two = lax.optimization_barrier(jnp.sum(second_f * dnorm_two, axis=0)) / row_total
    grad_one = (LOSS_SCALE * (dnorm_one - first_f * trace_one) / dev_one).astype(jnp.bfloat16)
    grad_two = (LOSS_SCALE * (dnorm_two - second_f * trace_two) / dev_two).astype(jnp.bfloat16)
    return (total_loss, grad_one, grad_two)
```

```python
import functools

import jax
import jax.numpy as jnp
from jax import lax
from jax.experimental import pallas as pl
from jax.experimental.pallas import tpu as pltpu
from jax.sharding import PartitionSpec as P

OFF_WEIGHT = 0.0051
EPSILON = 1e-05
LOSS_SCALE = 16.0
MESH = pl.DeviceIdType.MESH
F32 = jnp.float32
BF16 = jnp.bfloat16
STREAMS = 2
EXTRA = 16


def split_rows(values, width):
    row_ids = lax.broadcasted_iota(jnp.int32, (EXTRA, width), 0)
    block = jnp.zeros((EXTRA, width), F32)
    for k, value in enumerate(values):
        rest = value
        for part in range(3):
            piece = rest.astype(BF16).astype(F32)
            rest = rest - piece
            block = jnp.where(row_ids == 3 * k + part, piece, block)
    return block.astype(BF16)


def join_rows(block, count):
    wide = block.astype(F32)
    return [wide[3 * k : 3 * k + 1] + wide[3 * k + 1 : 3 * k + 2] + wide[3 * k + 2 : 3 * k + 3] for k in range(count)]


def stack_rows(values, width):
    row_ids = lax.broadcasted_iota(jnp.int32, (8, width), 0)
    block = jnp.zeros((8, width), F32)
    for k, value in enumerate(values):
        block = jnp.where(row_ids == k, value, block)
    return block


def kernel(
    xs, n, v1, v2, loss_o, g1_o, g2_o,
    raw1, raw2, n1f, n2f, own1, own2,
    st_a, st_b, st_xr, st_yr, tst_s, tst_r, sst_s, sst_r,
    acc, pst, pr, gx, gfull, sib_s, sib_r,
    rs_s, rs_r, ti_s, ti_r, ls_s, ls_r,
    t_sem, stx_sem, sty_sem, tst_sem, sst_sem, ag_ss, ag_rs, sb_ss, sb_rs,
    px_sem, gx_sem, sib_sem, rs_ss, rs_rs, ti_sem, ls_sem,
):
    rows, width = v1.shape
    half = n // 2
    srow = rows // STREAMS
    prow = width // xs
    total_rows = float(rows * n * xs)
    b, f = lax.axis_index("batch"), lax.axis_index("feat")
    x, y = lax.div(b, n), lax.rem(b, n)
    z, c = lax.div(f, 2), lax.rem(f, 2)
    o = 1 - c

    def dev(x_, y_, z_, c_):
        return (x_ * n + y_, z_ * 2 + c_)

    def wrap(v, m):
        return lax.rem(v + m, m)

    sibling = dev(x, y, z, o)
    partner = dev(x, z, y, c)
    x_peers = [dev(wrap(x + k, xs), y, z, c) for k in range(1, xs)]
    y_peers = [dev(x, wrap(y + k, n), z, c) for k in range(1, n)]
    ring = [
        [dev(x, wrap(y + 1, n), z, c), dev(x, wrap(y - 1, n), z, c)],
        [dev(x, y, wrap(z + 1, n), c), dev(x, y, wrap(z - 1, n), c)],
    ]
    pos = [y, z]
    off_diag = y != z
    on_diag = y == z

    def remote(src, dst, ss, rs, to):
        return pltpu.make_async_remote_copy(
            src_ref=src, dst_ref=dst, send_sem=ss, recv_sem=rs, device_id=to, device_id_type=MESH
        )

    barrier = pltpu.get_barrier_semaphore()
    greet = [sibling] + x_peers + y_peers + ring[1]
    for peer in greet:
        pl.semaphore_signal(barrier, inc=1, device_id=peer, device_id_type=MESH)

    @pl.when(off_diag)
    def _():
        pl.semaphore_signal(barrier, inc=1, device_id=partner, device_id_type=MESH)
        pl.semaphore_wait(barrier, len(greet) + 1)

    @pl.when(on_diag)
    def _():
        pl.semaphore_wait(barrier, len(greet))

    class Swap:
        def __init__(self, src, dst, sems):
            self.far = remote(src, dst, sems.at[0], sems.at[1], partner)
            self.near = pltpu.make_async_copy(src, dst, sems.at[1])

        def start(self):
            @pl.when(off_diag)
            def _():
                self.far.start()

            @pl.when(on_diag)
            def _():
                self.near.start()

        def wait_recv(self):
            @pl.when(off_diag)
            def _():
                self.far.wait_recv()

            @pl.when(on_diag)
            def _():
                self.near.wait()

        def wait_send(self):
            @pl.when(off_diag)
            def _():
                self.far.wait_send()

    swap = Swap(v2, raw2.at[c, y], t_sem)
    swap.start()
    late = []

    first, second = v1[...].astype(F32), v2[...].astype(F32)
    st_a[...] = stack_rows(
        [
            jnp.sum(first, axis=0, keepdims=True),
            jnp.sum(first * first, axis=0, keepdims=True),
            jnp.sum(second, axis=0, keepdims=True),
            jnp.sum(second * second, axis=0, keepdims=True),
        ],
        width,
    )
    stx = [remote(st_a, st_xr.at[k], stx_sem.at[0, k], stx_sem.at[1, k], to) for k, to in enumerate(x_peers)]
    for cp in stx:
        cp.start()

    def sib_copy(a, src, block, s, slot):
        sub = pl.ds(s * srow, srow)
        raw = (raw1, raw2)[a]
        return remote(src, raw.at[c, block, sub], sb_ss.at[a, slot, s], sb_rs.at[a, slot, s], sibling)

    def sib_recv(a, block, s, slot):
        sub = pl.ds(s * srow, srow)
        raw = (raw1, raw2)[a]
        return remote(raw.at[o, block, sub], raw.at[o, block, sub], sb_ss.at[a, slot, s], sb_rs.at[a, slot, s], sibling)

    for s in range(STREAMS):
        cp = sib_copy(0, v1.at[pl.ds(s * srow, srow)], y, s, 0)
        cp.start()
        late.append(cp)

    for cp in stx:
        cp.wait_recv()
    sums = st_a[...]
    for k in range(xs - 1):
        sums = sums + st_xr[k]
    st_b[...] = sums
    sty = [remote(st_b, st_yr.at[k], sty_sem.at[0, k], sty_sem.at[1, k], to) for k, to in enumerate(y_peers)]
    for cp in sty:
        cp.start()
    for cp in sty:
        cp.wait_recv()
    sums = st_b[...]
    for k in range(n - 1):
        sums = sums + st_yr[k]
    mean1, mean2 = sums[0:1] / total_rows, sums[2:3] / total_rows
    inv1 = 1.0 / jnp.sqrt(sums[1:2] / total_rows - mean1 * mean1 + EPSILON)
    inv2 = 1.0 / jnp.sqrt(sums[3:4] / total_rows - mean2 * mean2 + EPSILON)
    tst_s[...] = stack_rows([mean2, inv2], width)
    swap_st = Swap(tst_s, tst_r, tst_sem)
    swap_st.start()
    late += stx + sty

    def depth(d, s):
        return half if (s < STREAMS // 2) == (d == 0) else half - 1

    def ring_block(a, d, t):
        return wrap(pos[a] - t, n) if d == 0 else wrap(pos[a] + t, n)

    def ag_copy(a, d, t, s):
        sub = pl.ds(s * srow, srow)
        raw = (raw1, raw2)[a]
        block = ring_block(a, d, t)
        src = v1.at[sub] if (a == 0 and t == 0) else raw.at[c, block, sub]
        return remote(src, raw.at[c, block, sub], ag_ss.at[a, d, t, s], ag_rs.at[a, d, t, s], ring[a][d])

    for s in range(STREAMS):
        for d in range(2):
            if depth(d, s) > 0:
                cp = ag_copy(0, d, 0, s)
                cp.start()
                late.append(cp)
    own1[...] = ((first - mean1) * inv1).astype(BF16)
    own2[...] = ((second - mean2) * inv2).astype(BF16)
    swap.wait_recv()
    for s in range(STREAMS):
        for d in range(2):
            if depth(d, s) > 0:
                cp = ag_copy(1, d, 0, s)
                cp.start()
                late.append(cp)
        cp = sib_copy(1, raw2.at[c, z, pl.ds(s * srow, srow)], z, s, 0)
        cp.start()
        late.append(cp)

    def ring_slot(d, t):
        return 1 + t if d == 0 else 1 + half + t

    def forward(t):
        for s in range(STREAMS):
            for a in range(2):
                for d in range(2):
                    if t >= depth(d, s):
                        continue
                    ag_copy(a, d, t, s).wait_recv()
                    if t + 1 < depth(d, s):
                        cp = ag_copy(a, d, t + 1, s)
                        cp.start()
                        late.append(cp)
                    block = ring_block(a, d, t + 1)
                    cp = sib_copy(a, (raw1, raw2)[a].at[c, block, pl.ds(s * srow, srow)], block, s, ring_slot(d, t))
                    cp.start()
                    late.append(cp)

    forward(0)
    swap_st.wait_recv()
    mean2t, inv2t = tst_r[0:1], tst_r[1:2]
    sst_s[...] = stack_rows([mean1, inv1, mean2t, inv2t], width)
    sib_st = remote(sst_s, sst_r, sst_sem.at[0], sst_sem.at[1], sibling)
    sib_st.start()
    late.append(sib_st)
    for t in range(1, half):
        forward(t)
    sib_st.wait_recv()
    for a in range(2):
        for s in range(STREAMS):
            sib_recv(a, wrap(pos[a], n), s, 0).wait_recv()
            for d in range(2):
                for t in range(depth(d, s)):
                    sib_recv(a, ring_block(a, d, t + 1), s, ring_slot(d, t)).wait_recv()

    raw1[c, y] = v1[...]
    acc[...] = jnp.zeros_like(acc)

    def standard(i, _):
        n1f[c, i] = ((raw1[c, i].astype(F32) - mean1) * inv1).astype(BF16)
        n1f[o, i] = ((raw1[o, i].astype(F32) - sst_r[0:1]) * sst_r[1:2]).astype(BF16)
        n2f[c, i] = ((raw2[c, i].astype(F32) - mean2t) * inv2t).astype(BF16)
        n2f[o, i] = ((raw2[o, i].astype(F32) - sst_r[2:3]) * sst_r[3:4]).astype(BF16)
        for h in range(2):
            acc[h] += lax.dot_general(n1f[c, i], n2f[h, i], (((0,), (0,)), ((), ())), preferred_element_type=F32)
        return 0

    lax.fori_loop(0, n, standard, 0)

    row_ids = lax.broadcasted_iota(jnp.int32, (width, width), 0)
    col_ids = lax.broadcasted_iota(jnp.int32, (width, width), 1)
    diag_here = jnp.where(on_diag, 1.0, 0.0).astype(F32) / total_rows
    diag = jnp.sum(jnp.where(row_ids == col_ids, acc[c], 0.0), axis=0, keepdims=True) * diag_here
    extra = split_rows([diag], width)
    for k in range(xs):
        for h in range(2):
            pst[k, h, :prow] = (acc[h, k * prow : (k + 1) * prow] / total_rows).astype(BF16)
        pst[k, 0, prow:] = extra
        pst[k, 1, prow:] = extra
    px = [
        remote(pst.at[wrap(x + k, xs)], pr.at[k - 1], px_sem.at[0, k - 1], px_sem.at[1, k - 1], x_peers[k - 1])
        for k in range(1, xs)
    ]
    for cp in px:
        cp.start()
    late += px
    for cp in px:
        cp.wait_recv()
    for k in range(xs - 1):
        diag = diag + join_rows(pr[k, 0, prow:], 1)[0]
    diag_grad = (-2.0 * (1.0 - diag)).astype(BF16).astype(F32) * jnp.where(on_diag, 1.0, 0.0).astype(F32)
    prow_ids = lax.broadcasted_iota(jnp.int32, (prow, width), 0) + x * prow
    pcol_ids = lax.broadcasted_iota(jnp.int32, (prow, width), 1)
    same = prow_ids == pcol_ids
    loss = jnp.zeros((1, 1), F32)
    row_trace = jnp.zeros((prow, 1), F32)
    col_trace = []
    for h in range(2):
        corr = acc[h, pl.ds(pl.multiple_of(x * prow, prow), prow)] / total_rows
        for k in range(xs - 1):
            corr = corr + pr[k, h, :prow].astype(F32)
        spot = same & on_diag & (c == h)
        terms = jnp.where(spot, (1.0 - diag) * (1.0 - diag), OFF_WEIGHT * corr * corr)
        loss = loss + jnp.sum(jnp.sum(terms, axis=0, keepdims=True), axis=1, keepdims=True)
        grad = jnp.where(spot, 0.0, 2.0 * OFF_WEIGHT * corr).astype(BF16)
        gx[x, h, :prow] = grad
        share = corr * grad.astype(F32)
        row_trace = row_trace + jnp.sum(share, axis=1, keepdims=True)
        col_trace.append(jnp.sum(share, axis=0, keepdims=True))
    row_trace = jnp.sum(jnp.where(same, row_trace, 0.0), axis=0, keepdims=True)
    loss_row = jnp.zeros((1, width), F32) + loss
    gx[x, 0, prow:] = split_rows([col_trace[0], row_trace, loss_row], width)
    gx[x, 1, prow:] = split_rows([col_trace[1]], width)
    gc = [remote(gx.at[x], gx.at[x], gx_sem.at[0, k], gx_sem.at[1, k], to) for k, to in enumerate(x_peers)]
    for cp in gc:
        cp.start()
    for cp in late:
        cp.wait_send()
    swap.wait_send()
    swap_st.wait_send()
    for k in range(1, xs):
        src = wrap(x - k, xs)
        remote(gx.at[src], gx.at[src], gx_sem.at[0, k - 1], gx_sem.at[1, k - 1], x_peers[k - 1]).wait_recv()
    col0 = col1 = trace1 = loss_row = jnp.zeros((1, width), F32)
    for k in range(xs):
        for h in range(2):
            gfull[h, k * prow : (k + 1) * prow] = gx[k, h, :prow]
        part = join_rows(gx[k, 0, prow:], 3)
        col0, trace1, loss_row = col0 + part[0], trace1 + part[1], loss_row + part[2]
        col1 = col1 + join_rows(gx[k, 1, prow:], 1)[0]
    is_low = c == 0
    mine = jnp.where(is_low, col0, col1)
    theirs = jnp.where(is_low, col1, col0)
    diag_trace = diag * diag_grad
    trace1 = trace1 + diag_trace
    trace2 = mine + diag_trace

    sib_s[:width] = gfull[o]
    sib_s[width:] = split_rows([theirs, loss_row], width)
    sib = remote(sib_s, sib_r, sib_sem.at[0], sib_sem.at[1], sibling)
    sib.start()
    late = gc + [sib]
    sib.wait_recv()
    part = join_rows(sib_r[width:], 2)
    trace2 = trace2 + part[0]
    loss_row = loss_row + part[1]

    ring_extra = [[trace1, diag_grad], [trace2, loss_row]]

    def product(a, block, s):
        sub = pl.ds(s * srow, srow)
        if a == 0:
            dims = (((1,), (1,)), ((), ()))
            left, right = (n2f[0, block, sub], n2f[1, block, sub]), (gfull[0], gfull[1])
        else:
            dims = (((1,), (0,)), ((), ()))
            left, right = (n1f[c, block, sub], n1f[o, block, sub]), (gfull[c], sib_r[:width])
        return lax.dot_general(left[0], right[0], dims, preferred_element_type=F32) + lax.dot_general(
            left[1], right[1], dims, preferred_element_type=F32
        )

    def rs_copy(a, d, t, s):
        sub = pl.ds(0, srow + (EXTRA if s == 0 else 0))
        return remote(
            rs_s.at[a, d, t, s, sub], rs_r.at[a, d, t, s, sub], rs_ss.at[a, d, t, s], rs_rs.at[a, d, t, s], ring[a][d]
        )

    for t in range(half):
        for s in range(STREAMS):
            for a in range(2):
                for d in range(2):
                    deep = depth(d, s)
                    if t >= deep:
                        continue
                    block = ring_block(a, 1 - d, deep - t)
                    value = product(a, block, s)
                    if t > 0:
                        rs_copy(a, d, t - 1, s).wait_recv()
                        value = value + rs_r[a, d, t - 1, s, :srow].astype(F32)
                    rs_s[a, d, t, s, :srow] = value.astype(BF16)
                    if s == 0:
                        carried = ring_extra[a]
                        if t > 0:
                            got = join_rows(rs_r[a, d, t - 1, s, srow:], 2)
                            carried = [u + w for u, w in zip(carried, got)]
                        rs_s[a, d, t, s, srow:] = split_rows(carried, width)
                    cp = rs_copy(a, d, t, s)
                    cp.start()
                    late.append(cp)

    def finish(a, s):
        value = product(a, pos[a], s)
        carried = ring_extra[a]
        for d in range(2):
            deep = depth(d, s)
            if deep == 0:
                continue
            rs_copy(a, d, deep - 1, s).wait_recv()
            value = value + rs_r[a, d, deep - 1, s, :srow].astype(F32)
            if s == 0:
                got = join_rows(rs_r[a, d, deep - 1, s, srow:], 2)
                carried = [u + w for u, w in zip(carried, got)]
        return value, carried

    backs = []
    for s in range(STREAMS):
        value, carried = finish(1, s)
        ti_s[s, :srow] = value.astype(BF16)
        if s == 0:
            trace2, loss_row = carried
            ti_s[s, srow:] = split_rows([trace2], width)
        else:
            ti_s[s, srow:] = jnp.zeros((EXTRA, width), BF16)
        back = Swap(ti_s.at[s], ti_r.at[s], ti_sem.at[s])
        back.start()
        backs.append(back)
    ls_s[...] = jnp.zeros((8, width), F32) + loss_row
    lc = [remote(ls_s, ls_r.at[k], ls_sem.at[0, k], ls_sem.at[1, k], to) for k, to in enumerate(y_peers)]
    for cp in lc:
        cp.start()
    late += lc
    for s in range(STREAMS):
        value, carried = finish(0, s)
        if s == 0:
            trace1, diag_grad = carried
        sub = pl.ds(s * srow, srow)
        value = value + own2[sub].astype(F32) * diag_grad - own1[sub].astype(F32) * trace1
        g1_o[sub] = (LOSS_SCALE * value * inv1).astype(BF16)
    for cp in late:
        cp.wait_send()
    for cp in lc:
        cp.wait_recv()
    for k in range(n - 1):
        loss_row = loss_row + ls_r[k, 0:1]
    loss_o[...] = loss_row[:, 0:1]
    for s in range(STREAMS):
        backs[s].wait_recv()
        if s == 0:
            trace2 = join_rows(ti_r[0, srow:], 1)[0]
        sub = pl.ds(s * srow, srow)
        value = ti_r[s, :srow].astype(F32) + own1[sub].astype(F32) * diag_grad - own2[sub].astype(F32) * trace2
        g2_o[sub] = (LOSS_SCALE * value * inv2).astype(BF16)
    for back in backs:
        back.wait_send()


def on_device(xs, n, view_one, view_two):
    rows, width = view_one.shape
    half = n // 2
    srow = rows // STREAMS
    prow = width // xs
    sem = pltpu.SemaphoreType.DMA
    blocks = (2, n, rows, width)
    ring = (2, 2, half, STREAMS)
    loss, grad_one, grad_two = pl.pallas_call(
        functools.partial(kernel, xs, n),
        out_shape=(
            jax.ShapeDtypeStruct((1, 1), F32),
            jax.ShapeDtypeStruct((rows, width), BF16),
            jax.ShapeDtypeStruct((rows, width), BF16),
        ),
        in_specs=[pl.BlockSpec(memory_space=pltpu.VMEM)] * 2,
        out_specs=[pl.BlockSpec(memory_space=pltpu.VMEM)] * 3,
        scratch_shapes=[
            pltpu.VMEM(blocks, BF16),
            pltpu.VMEM(blocks, BF16),
            pltpu.VMEM(blocks, BF16),
            pltpu.VMEM(blocks, BF16),
            pltpu.VMEM((rows, width), BF16),
            pltpu.VMEM((rows, width), BF16),
            pltpu.VMEM((8, width), F32),
            pltpu.VMEM((8, width), F32),
            pltpu.VMEM((xs - 1, 8, width), F32),
            pltpu.VMEM((n - 1, 8, width), F32),
            pltpu.VMEM((8, width), F32),
            pltpu.VMEM((8, width), F32),
            pltpu.VMEM((8, width), F32),
            pltpu.VMEM((8, width), F32),
            pltpu.VMEM((2, width, width), F32),
            pltpu.VMEM((xs, 2, prow + EXTRA, width), BF16),
            pltpu.VMEM((xs - 1, 2, prow + EXTRA, width), BF16),
            pltpu.VMEM((xs, 2, prow + EXTRA, width), BF16),
            pltpu.VMEM((2, width, width), BF16),
            pltpu.VMEM((width + EXTRA, width), BF16),
            pltpu.VMEM((width + EXTRA, width), BF16),
            pltpu.VMEM(ring + (srow + EXTRA, width), BF16),
            pltpu.VMEM(ring + (srow + EXTRA, width), BF16),
            pltpu.VMEM((STREAMS, srow + EXTRA, width), BF16),
            pltpu.VMEM((STREAMS, srow + EXTRA, width), BF16),
            pltpu.VMEM((8, width), F32),
            pltpu.VMEM((n - 1, 8, width), F32),
            sem((2,)),
            sem((2, xs - 1)),
            sem((2, n - 1)),
            sem((2,)),
            sem((2,)),
            sem(ring),
            sem(ring),
            sem((2, n + 1, STREAMS)),
            sem((2, n + 1, STREAMS)),
            sem((2, xs - 1)),
            sem((2, xs - 1)),
            sem((2,)),
            sem(ring),
            sem(ring),
            sem((STREAMS, 2)),
            sem((2, n - 1)),
        ],
        compiler_params=pltpu.CompilerParams(
            collective_id=0, has_side_effects=True, vmem_limit_bytes=40 * 2**20
        ),
        name="barlow",
    )(view_one, view_two)
    return loss.reshape(()), grad_one, grad_two


def solution(mesh):
    n = mesh.shape["feat"] // 2
    xs = mesh.shape["batch"] // n
    spec = P("batch", "feat")
    return jax.shard_map(
        functools.partial(on_device, xs, n),
        mesh=mesh,
        in_specs=(spec, spec),
        out_specs=(P(), spec, spec),
        check_vma=False,
    )
```

```python
import functools

import jax
import jax.numpy as jnp
from jax import lax
from jax.experimental import pallas as pl
from jax.experimental.pallas import tpu as pltpu
from jax.sharding import PartitionSpec as P

OFF_WEIGHT = 0.0051
EPSILON = 1e-05
LOSS_SCALE = 16.0
MESH = pl.DeviceIdType.MESH
F32 = jnp.float32
BF16 = jnp.bfloat16
STREAMS = 2
EXTRA = 16


def split_rows(values, width):
    row_ids = lax.broadcasted_iota(jnp.int32, (EXTRA, width), 0)
    block = jnp.zeros((EXTRA, width), F32)
    for k, value in enumerate(values):
        rest = value
        for part in range(3):
            piece = rest.astype(BF16).astype(F32)
            rest = rest - piece
            block = jnp.where(row_ids == 3 * k + part, piece, block)
    return block.astype(BF16)


def join_rows(block, count):
    wide = block.astype(F32)
    return [wide[3 * k : 3 * k + 1] + wide[3 * k + 1 : 3 * k + 2] + wide[3 * k + 2 : 3 * k + 3] for k in range(count)]


def stack_rows(values, width):
    row_ids = lax.broadcasted_iota(jnp.int32, (8, width), 0)
    block = jnp.zeros((8, width), F32)
    for k, value in enumerate(values):
        block = jnp.where(row_ids == k, value, block)
    return block


def kernel(
    xs, n, v1, v2, loss_o, g1_o, g2_o,
    raw1, raw2, n1f, n2f, own2, hop_a, hop_b, ssum, qsum, tst_s, tst_r, tr_s, tr_r,
    acc, pst, pr, gx, gfull, sib_s, sib_r,
    rs_s, rs_r, ti_s, ti_r, ls_s, ls_r,
    in_sem, t_sem, tst_sem, tr_sem, ag_ss, ag_rs, sb_ss, sb_rs,
    px_sem, gx_sem, sib_sem, rs_ss, rs_rs, ti_sem, ls_sem,
):
    rows, width = v1.shape
    half = n // 2
    srow = rows // STREAMS
    prow = width // xs
    part_rows = rows // n
    group_rows = float(rows * n)
    total_rows = float(rows * n * xs)
    b, f = lax.axis_index("batch"), lax.axis_index("feat")
    x, y = lax.div(b, n), lax.rem(b, n)
    z, c = lax.div(f, 2), lax.rem(f, 2)
    o = 1 - c
    is_low = c == 0
    skip = half == 4

    def dev(x_, y_, z_, c_):
        return (x_ * n + y_, z_ * 2 + c_)

    def wrap(v, m):
        return lax.rem(v + m, m)

    sibling = dev(x, y, z, o)
    partner = dev(x, z, y, c)
    x_peers = [dev(wrap(x + k, xs), y, z, c) for k in range(1, xs)]
    y_peers = [dev(x, wrap(y + k, n), z, c) for k in range(1, n)]
    z_peers = [dev(x, y, wrap(z + k, n), c) for k in range(1, n)]
    nearest = sorted(range(1, n), key=lambda k: min(k, n - k))

    def along(a, k):
        return dev(x, wrap(y + k, n), z, c) if a == 0 else dev(x, y, wrap(z + k, n), c)

    ring = [[along(a, 1), along(a, -1)] for a in range(2)]
    ring2 = [[along(a, 2), along(a, -2)] for a in range(2)] if skip else None
    pos = [y, z]
    off_diag = y != z
    on_diag = y == z
    diag_one = jnp.where(on_diag, 1.0, 0.0).astype(F32)

    def remote(src, dst, ss, rs, to):
        return pltpu.make_async_remote_copy(
            src_ref=src, dst_ref=dst, send_sem=ss, recv_sem=rs, device_id=to, device_id_type=MESH
        )

    def stream(s):
        return pl.ds(s * srow, srow)

    load1 = pltpu.make_async_copy(v1, raw1.at[c, y], in_sem.at[0])
    load2 = pltpu.make_async_copy(v2, own2, in_sem.at[1])
    load1.start()
    load2.start()
    barrier = pltpu.get_barrier_semaphore()
    greet = [sibling] + x_peers + y_peers + z_peers
    for peer in greet:
        pl.semaphore_signal(barrier, inc=1, device_id=peer, device_id_type=MESH)

    @pl.when(off_diag)
    def _():
        pl.semaphore_signal(barrier, inc=1, device_id=partner, device_id_type=MESH)

    load1.wait()
    load2.wait()

    @pl.when(off_diag)
    def _():
        pl.semaphore_wait(barrier, len(greet) + 1)

    @pl.when(on_diag)
    def _():
        pl.semaphore_wait(barrier, len(greet))

    class Swap:
        def __init__(self, src, dst, sems):
            self.far = remote(src, dst, sems.at[0], sems.at[1], partner)
            self.near = pltpu.make_async_copy(src, dst, sems.at[1])

        def start(self):
            @pl.when(off_diag)
            def _():
                self.far.start()

            @pl.when(on_diag)
            def _():
                self.near.start()

        def wait_recv(self):
            @pl.when(off_diag)
            def _():
                self.far.wait_recv()

            @pl.when(on_diag)
            def _():
                self.near.wait()

        def wait_send(self):
            @pl.when(off_diag)
            def _():
                self.far.wait_send()

    late = []

    def go(cp):
        cp.start()
        late.append(cp)

    def part(k):
        return pl.ds(pl.multiple_of(k * part_rows, part_rows), part_rows)

    class Exchange:
        def __init__(self, source, hop, target, sems, along_z):
            self.source, self.hop, self.target, self.sems = source, hop, target, sems
            self.peers = z_peers if along_z else y_peers
            self.here, self.there = (z, y) if along_z else (y, z)
            self.to = (lambda k: dev(x, k, z, c)) if along_z else (lambda k: dev(x, y, k, c))

        def first(self, k):
            hop_ref = self.hop.at[self.here]
            return remote(
                self.source(wrap(self.here + k, n)), hop_ref, self.sems.at[0, k], self.sems.at[1, k], self.peers[k - 1]
            )

        def stay(self):
            return pltpu.make_async_copy(self.source(self.here), self.hop.at[self.here], self.sems.at[1, 0])

        def second(self, k):
            origin = wrap(self.here - k, n)
            far = remote(
                self.hop.at[origin], self.target(self.there), self.sems.at[2, k], self.sems.at[3, self.there], self.to(origin)
            )
            near = pltpu.make_async_copy(self.hop.at[origin], self.target(self.there), self.sems.at[3, self.there])
            return origin, far, near

        def start(self):
            self.stay().start()
            for k in nearest:
                self.first(k).start()

        def pass_on(self, some):
            for k in some:
                if k == 0:
                    self.stay().wait()
                else:
                    self.first(k).wait_recv()
                origin, far, near = self.second(k)

                @pl.when(origin != self.there)
                def _():
                    far.start()

                @pl.when(origin == self.there)
                def _():
                    near.start()

        def wait_recv(self):
            for k in [0] + nearest:
                came = wrap(self.there + k, n)
                ref = self.target(came)
                if k == 0:
                    pltpu.make_async_copy(ref, ref, self.sems.at[3, came]).wait()
                else:
                    remote(ref, ref, self.sems.at[2, k], self.sems.at[3, came], self.peers[0]).wait_recv()

        def wait_send(self):
            for k in nearest:
                self.first(k).wait_send()
            for k in range(n):
                origin, far, _ = self.second(k)

                @pl.when(origin != self.there)
                def _():
                    far.wait_send()

    spread_out = Exchange(lambda k: own2.at[part(k)], hop_a, lambda k: raw2.at[c, k, part(z)], t_sem, True)
    spread_out.start()

    raws, norms = (raw1, raw2), (n1f, n2f)

    def depth(d, s):
        return half if (s < STREAMS // 2) == (d == 0) else half - 1

    def ring_block(a, d, t):
        return wrap(pos[a] - t, n) if d == 0 else wrap(pos[a] + t, n)

    def piece(a, core, block, s):
        if a == 0:
            return raw1.at[core, block, stream(s)]
        return raw2.at[core, pl.ds(s * n // STREAMS, n // STREAMS), part(block)]

    def block_of(refs, a, core, block):
        if a == 0:
            return refs[core, block]
        return refs[core, :, part(block)].reshape(rows, width)

    def ag_copy(a, d, t, s):
        far = skip and t == 3
        block = ring_block(a, d, 2 if far else t)
        ref = piece(a, c, block, s)
        return remote(ref, ref, ag_ss.at[a, d, t, s], ag_rs.at[a, d, t, s], (ring2 if far else ring)[a][d])

    def sib_copy(a, core, block, s, slot):
        ref = piece(a, core, block, s)
        return remote(ref, ref, sb_ss.at[a, slot, s], sb_rs.at[a, slot, s], sibling)

    def ring_slot(d, t):
        return 1 + t if d == 0 else 1 + half + t

    def open_ring(a, s):
        for d in range(2):
            if depth(d, s) > 0:
                go(ag_copy(a, d, 0, s))
        go(sib_copy(a, c, pos[a], s, 0))

    def forward(a, t):
        for s in range(STREAMS):
            for d in range(2):
                if t >= depth(d, s):
                    continue
                ag_copy(a, d, t, s).wait_recv()
                if t + 1 < min(depth(d, s), 3 if skip else half):
                    go(ag_copy(a, d, t + 1, s))
                if skip and t == 1 and depth(d, s) == 4:
                    go(ag_copy(a, d, 3, s))
                go(sib_copy(a, c, ring_block(a, d, t + 1), s, ring_slot(d, t)))

    def sib_wait(a, s, d, t):
        if d is None:
            sib_copy(a, o, pos[a], s, 0).wait_recv()
        elif t < depth(d, s):
            sib_copy(a, o, ring_block(a, d, t + 1), s, ring_slot(d, t)).wait_recv()

    shifts = {}

    def fold(value):
        return jnp.sum(value.reshape(rows // 8, 8, width), axis=0)

    def shifted(a, block, begin):
        for h, core in enumerate((c, o)):
            value = block_of(raws[a], a, core, block).astype(F32)
            if begin:
                shifts[a, h] = jnp.sum(fold(value), axis=0, keepdims=True) / rows
            value = value - shifts[a, h]
            if a == 0:
                norms[a][core, block] = value.astype(BF16)
            else:
                norms[a][core, :, part(block)] = value.astype(BF16).reshape(n, part_rows, width)
            if begin:
                ssum[a, h] = fold(value)
                qsum[a, h] = fold(value * value)
            else:
                ssum[a, h] += fold(value)
                qsum[a, h] += fold(value * value)

    def correlate(block, begin):
        for h in range(2):
            share = lax.dot_general(
                block_of(n1f, 1, c, block), block_of(n2f, 1, h, block), (((0,), (0,)), ((), ())), preferred_element_type=F32
            )
            if begin:
                acc[h] = share
            else:
                acc[h] += share

    def arrived(a, t):
        if t + 1 < half:
            blocks = [ring_block(a, 0, t + 1), ring_block(a, 1, t + 1)]
        else:
            blocks = [ring_block(a, 0, half)]
        for s in range(STREAMS):
            for d in range(2):
                sib_wait(a, s, d, t)
        for block in blocks:
            shifted(a, block, False)
            if a == 1:
                correlate(block, False)

    for s in range(STREAMS):
        open_ring(0, s)
    spread_out.pass_on([0] + nearest)
    spread_out.wait_recv()
    for s in range(STREAMS):
        open_ring(1, s)
    for s in range(STREAMS):
        sib_wait(0, s, None, 0)
    shifted(0, y, True)
    forward(0, 0)
    forward(1, 0)
    for s in range(STREAMS):
        sib_wait(1, s, None, 0)
    shifted(1, z, True)
    for t in range(1, half):
        forward(0, t)
        forward(1, t)
        arrived(0, t - 1)
        if t == 1 and half > 1:
            pass
    arrived(0, half - 1)
    correlate(z, True)
    for t in range(half):
        arrived(1, t)

    def spread(row, count, first):
        ids = lax.broadcasted_iota(jnp.int32, (count, width), 0) + first
        lanes = lax.broadcasted_iota(jnp.int32, (count, width), 1)
        return jnp.sum(jnp.where(ids == lanes, row, 0.0), axis=1, keepdims=True)

    rests, means, squares = {}, {}, {}
    for a in range(2):
        for h in range(2):
            rest = jnp.sum(ssum[a, h], axis=0, keepdims=True) / group_rows
            rests[a, h] = rest
            means[a, h] = shifts[a, h] + rest
            squares[a, h] = jnp.sum(qsum[a, h], axis=0, keepdims=True) - group_rows * rest * rest

    def by_half(table, a):
        return [jnp.where(is_low, table[a, 0], table[a, 1]), jnp.where(is_low, table[a, 1], table[a, 0])]

    rest2, mean2, square2 = by_half(rests, 1), by_half(means, 1), by_half(squares, 1)
    column = spread(rests[0, 0], width, 0) * (group_rows / total_rows)
    row_ids = lax.broadcasted_iota(jnp.int32, (width, width), 0)
    col_ids = lax.broadcasted_iota(jnp.int32, (width, width), 1)
    for h in range(2):
        acc[h] = acc[h] / total_rows - column * rest2[h]
    diag = jnp.sum(jnp.where(row_ids == col_ids, acc[c], 0.0), axis=0, keepdims=True) * diag_one
    facts = [
        [means[0, 0], squares[0, 0], mean2[0], square2[0], diag],
        [means[0, 1], squares[0, 1], mean2[1], square2[1]],
    ]

    for h in range(2):
        extra = split_rows(facts[h], width)
        for k in range(xs):
            pst[k, h, :prow] = acc[h, k * prow : (k + 1) * prow].astype(BF16)
            pst[k, h, prow:] = extra
    px = [
        remote(pst.at[wrap(x + k, xs)], pr.at[k - 1], px_sem.at[0, k - 1], px_sem.at[1, k - 1], x_peers[k - 1])
        for k in range(1, xs)
    ]
    for cp in px:
        go(cp)
    for cp in px:
        cp.wait_recv()
    every = [facts]
    for k in range(xs - 1):
        every.append([join_rows(pr[k, 0, prow:], 5), join_rows(pr[k, 1, prow:], 4)])

    def whole(h, place):
        center = sum(e[h][place] for e in every) / xs
        spreads = [e[h][place] - center for e in every]
        square = sum(e[h][place + 1] for e in every) + group_rows * sum(v * v for v in spreads)
        return center, 1.0 / jnp.sqrt(square / total_rows + EPSILON), spreads

    center1, inv1, spread1 = whole(0, 0)
    center1o, inv1o, _ = whole(1, 0)
    center2, inv2, spread2 = [[v[h] for h in range(2)] for v in zip(*[whole(h, 2) for h in range(2)])]
    near2 = [jnp.where(is_low, v[0], v[1]) for v in (center2, inv2)]
    near_spread2 = [jnp.where(is_low, u, w) for u, w in zip(*spread2)]
    tst_s[...] = stack_rows(near2, width)
    swap_st = Swap(tst_s, tst_r, tst_sem)
    swap_st.start()

    diag = sum(e[0][4] for e in every) + sum(u * w for u, w in zip(spread1, near_spread2)) / xs * diag_one
    diag = diag * inv1 * near2[1]
    diag_grad = (-2.0 * (1.0 - diag)).astype(BF16).astype(F32) * diag_one
    prow_ids = lax.broadcasted_iota(jnp.int32, (prow, width), 0) + x * prow
    pcol_ids = lax.broadcasted_iota(jnp.int32, (prow, width), 1)
    same = prow_ids == pcol_ids
    inv_column = spread(inv1, prow, x * prow)
    spread_columns = [spread(v, prow, x * prow) / xs for v in spread1]
    loss = jnp.zeros((1, 1), F32)
    row_trace = jnp.zeros((prow, 1), F32)
    col_trace = []
    for h in range(2):
        corr = acc[h, pl.ds(pl.multiple_of(x * prow, prow), prow)]
        for k in range(xs - 1):
            corr = corr + pr[k, h, :prow].astype(F32)
        for k in range(xs):
            corr = corr + spread_columns[k] * spread2[h][k]
        corr = corr * inv_column * inv2[h]
        spot = same & on_diag & (c == h)
        terms = jnp.where(spot, (1.0 - diag) * (1.0 - diag), OFF_WEIGHT * corr * corr)
        loss = loss + jnp.sum(jnp.sum(terms, axis=0, keepdims=True), axis=1, keepdims=True)
        grad = jnp.where(spot, 0.0, 2.0 * OFF_WEIGHT * corr).astype(BF16)
        gx[x, h, :prow] = grad
        share = corr * grad.astype(F32)
        row_trace = row_trace + jnp.sum(share, axis=1, keepdims=True)
        col_trace.append(jnp.sum(share, axis=0, keepdims=True))
    row_trace = jnp.sum(jnp.where(same, row_trace, 0.0), axis=0, keepdims=True)
    loss_row = jnp.zeros((1, width), F32) + loss
    gx[x, 0, prow:] = split_rows([col_trace[0], row_trace, loss_row], width)
    gx[x, 1, prow:] = split_rows([col_trace[1]], width)
    gc = [remote(gx.at[x], gx.at[x], gx_sem.at[0, k], gx_sem.at[1, k], to) for k, to in enumerate(x_peers)]
    for cp in gc:
        cp.start()

    def standard(i, _):
        n1f[c, i] = ((raw1[c, i].astype(F32) - center1) * inv1).astype(BF16)
        n1f[o, i] = ((raw1[o, i].astype(F32) - center1o) * inv1o).astype(BF16)
        for h in range(2):
            n2f[h, i] = ((raw2[h, i].astype(F32) - center2[h]) * inv2[h]).astype(BF16)
        return 0

    lax.fori_loop(0, n, standard, 0)
    for cp in late:
        cp.wait_send()
    spread_out.wait_send()
    swap_st.wait_send()
    for k in range(1, xs):
        src = wrap(x - k, xs)
        remote(gx.at[src], gx.at[src], gx_sem.at[0, k - 1], gx_sem.at[1, k - 1], x_peers[k - 1]).wait_recv()
    col0 = col1 = trace1 = loss_row = jnp.zeros((1, width), F32)
    for k in range(xs):
        for h in range(2):
            gfull[h, k * prow : (k + 1) * prow] = gx[k, h, :prow]
        got = join_rows(gx[k, 0, prow:], 3)
        col0, trace1, loss_row = col0 + got[0], trace1 + got[1], loss_row + got[2]
        col1 = col1 + join_rows(gx[k, 1, prow:], 1)[0]
    mine = jnp.where(is_low, col0, col1)
    theirs = jnp.where(is_low, col1, col0)
    diag_trace = diag * diag_grad
    trace1 = trace1 + diag_trace
    trace2 = mine + diag_trace

    sib_s[:width] = gfull[o]
    sib_s[width:] = split_rows([theirs, loss_row], width)
    sib = remote(sib_s, sib_r, sib_sem.at[0], sib_sem.at[1], sibling)
    sib.start()
    late = gc + [sib]
    sib.wait_recv()
    got = join_rows(sib_r[width:], 2)
    trace2 = trace2 + got[0]
    loss_row = loss_row + got[1]

    ring_extra = [[trace1, diag_grad], [trace2, loss_row]]

    def product(a, block, s):
        if a == 0:
            dims = (((1,), (1,)), ((), ()))
            left, right = [n2f[h, block, stream(s)] for h in range(2)], (gfull[0], gfull[1])
        else:
            dims = (((1,), (0,)), ((), ()))
            images = pl.ds(s * n // STREAMS, n // STREAMS)
            left = [n1f[h, images, part(block)].reshape(srow, width) for h in (c, o)]
            right = (gfull[c], sib_r[:width])
        return lax.dot_general(left[0], right[0], dims, preferred_element_type=F32) + lax.dot_general(
            left[1], right[1], dims, preferred_element_type=F32
        )

    def rs_copy(a, d, t, s):
        far = skip and t == 0 and depth(d, s) == 4
        sub = pl.ds(0, srow + (EXTRA if s == 0 else 0))
        return remote(
            rs_s.at[a, d, t, s, sub], rs_r.at[a, d, t, s, sub], rs_ss.at[a, d, t, s], rs_rs.at[a, d, t, s],
            (ring2 if far else ring)[a][d],
        )

    def takes(d, t, s):
        if skip and depth(d, s) == 4:
            return {0: [], 1: [], 2: [0, 1], 3: [2]}[t]
        return [t - 1] if t > 0 else []

    def add_in(a, d, s, value, carried, messages):
        for m in messages:
            rs_copy(a, d, m, s).wait_recv()
            value = value + rs_r[a, d, m, s, :srow].astype(F32)
            if s == 0:
                got = join_rows(rs_r[a, d, m, s, srow:], 2)
                carried = [u + w for u, w in zip(carried, got)]
        return value, carried

    def rs_send(a, d, t, s):
        block = ring_block(a, 1 - d, depth(d, s) - t)
        value, carried = add_in(a, d, s, product(a, block, s), ring_extra[a], takes(d, t, s))
        rs_s[a, d, t, s, :srow] = value.astype(BF16)
        if s == 0:
            rs_s[a, d, t, s, srow:] = split_rows(carried, width)
        go(rs_copy(a, d, t, s))

    lanes = [(s, a, d) for s in range(STREAMS) for a in range(2) for d in range(2)]
    for step in range(half):
        for s, a, d in lanes:
            deep = depth(d, s)
            if skip and deep == 4:
                for t in ([0, 1], [2], [3], [])[step]:
                    rs_send(a, d, t, s)
            elif step < deep:
                rs_send(a, d, step, s)

    def finish(a, s):
        value, carried = product(a, pos[a], s), ring_extra[a]
        for d in range(2):
            if depth(d, s) > 0:
                value, carried = add_in(a, d, s, value, carried, [depth(d, s) - 1])
        return value, carried

    for s in range(STREAMS):
        value, carried = finish(1, s)
        ti_s[pl.ds(s * n // STREAMS, n // STREAMS)] = value.astype(BF16).reshape(n // STREAMS, part_rows, width)
        if s == 0:
            trace2, loss_row = carried
    come_back = Exchange(lambda k: ti_s.at[k], hop_b, lambda k: ti_r.at[part(k)], ti_sem, False)
    come_back.start()
    tr_s[...] = stack_rows([trace2], width)
    swap_tr = Swap(tr_s, tr_r, tr_sem)
    swap_tr.start()
    swap_st.wait_recv()
    far_center, far_inv = tst_r[0:1], tst_r[1:2]
    second = ((own2[...].astype(F32) - far_center) * far_inv).astype(BF16)
    own2[...] = second
    come_back.pass_on([0] + nearest)
    ls_s[...] = jnp.zeros((8, width), F32) + loss_row
    lc = [remote(ls_s, ls_r.at[k], ls_sem.at[0, k], ls_sem.at[1, k], to) for k, to in enumerate(y_peers)]
    for cp in lc:
        go(cp)
    for s in range(STREAMS):
        value, carried = finish(0, s)
        if s == 0:
            trace1, diag_grad = carried
        value = value + own2[stream(s)].astype(F32) * diag_grad - n1f[c, y, stream(s)].astype(F32) * trace1
        g1_o[stream(s)] = (LOSS_SCALE * value * inv1).astype(BF16)
    for cp in late:
        cp.wait_send()
    for cp in lc:
        cp.wait_recv()
    for k in range(n - 1):
        loss_row = loss_row + ls_r[k, 0:1]
    loss_o[...] = loss_row[:, 0:1]
    swap_tr.wait_recv()
    trace2 = tr_r[0:1]
    come_back.wait_recv()
    value = ti_r[...].astype(F32) + n1f[c, y].astype(F32) * diag_grad - own2[...].astype(F32) * trace2
    g2_o[...] = (LOSS_SCALE * value * far_inv).astype(BF16)
    come_back.wait_send()
    swap_tr.wait_send()


def on_device(xs, n, view_one, view_two):
    rows, width = view_one.shape
    half = n // 2
    srow = rows // STREAMS
    prow = width // xs
    sem = pltpu.SemaphoreType.DMA
    blocks = (2, n, rows, width)
    ring = (2, 2, half, STREAMS)
    loss, grad_one, grad_two = pl.pallas_call(
        functools.partial(kernel, xs, n),
        out_shape=(
            jax.ShapeDtypeStruct((1, 1), F32),
            jax.ShapeDtypeStruct((rows, width), BF16),
            jax.ShapeDtypeStruct((rows, width), BF16),
        ),
        in_specs=[pl.BlockSpec(memory_space=pl.ANY)] * 2,
        out_specs=[pl.BlockSpec(memory_space=pltpu.VMEM)] * 3,
        scratch_shapes=[
            pltpu.VMEM(blocks, BF16),
            pltpu.VMEM(blocks, BF16),
            pltpu.VMEM(blocks, BF16),
            pltpu.VMEM(blocks, BF16),
            pltpu.VMEM((rows, width), BF16),
            pltpu.VMEM((n, rows // n, width), BF16),
            pltpu.VMEM((n, rows // n, width), BF16),
            pltpu.VMEM((2, 2, 8, width), F32),
            pltpu.VMEM((2, 2, 8, width), F32),
            pltpu.VMEM((8, width), F32),
            pltpu.VMEM((8, width), F32),
            pltpu.VMEM((8, width), F32),
            pltpu.VMEM((8, width), F32),
            pltpu.VMEM((2, width, width), F32),
            pltpu.VMEM((xs, 2, prow + EXTRA, width), BF16),
            pltpu.VMEM((xs - 1, 2, prow + EXTRA, width), BF16),
            pltpu.VMEM((xs, 2, prow + EXTRA, width), BF16),
            pltpu.VMEM((2, width, width), BF16),
            pltpu.VMEM((width + EXTRA, width), BF16),
            pltpu.VMEM((width + EXTRA, width), BF16),
            pltpu.VMEM(ring + (srow + EXTRA, width), BF16),
            pltpu.VMEM(ring + (srow + EXTRA, width), BF16),
            pltpu.VMEM((n, rows // n, width), BF16),
            pltpu.VMEM((rows, width), BF16),
            pltpu.VMEM((8, width), F32),
            pltpu.VMEM((n - 1, 8, width), F32),
            sem((2,)),
            sem((4, n)),
            sem((2,)),
            sem((2,)),
            sem(ring),
            sem(ring),
            sem((2, n + 1, STREAMS)),
            sem((2, n + 1, STREAMS)),
            sem((2, xs - 1)),
            sem((2, xs - 1)),
            sem((2,)),
            sem(ring),
            sem(ring),
            sem((4, n)),
            sem((2, n - 1)),
        ],
        compiler_params=pltpu.CompilerParams(
            collective_id=0, has_side_effects=True, vmem_limit_bytes=40 * 2**20
        ),
        name="barlow",
    )(view_one, view_two)
    return loss.reshape(()), grad_one, grad_two


def solution(mesh):
    n = mesh.shape["feat"] // 2
    xs = mesh.shape["batch"] // n
    spec = P("batch", "feat")
    return jax.shard_map(
        functools.partial(on_device, xs, n),
        mesh=mesh,
        in_specs=(spec, spec),
        out_specs=(P(), spec, spec),
        check_vma=False,
    )
```

```python
import functools

import jax
import jax.numpy as jnp
from jax import lax
from jax.experimental import pallas as pl
from jax.experimental.pallas import tpu as pltpu
from jax.sharding import PartitionSpec as P

OFF_WEIGHT = 0.0051
EPSILON = 1e-05
LOSS_SCALE = 16.0
MESH = pl.DeviceIdType.MESH
F32 = jnp.float32
BF16 = jnp.bfloat16
STREAMS = 2
EXTRA = 16


def split_rows(values, width):
    row_ids = lax.broadcasted_iota(jnp.int32, (EXTRA, width), 0)
    block = jnp.zeros((EXTRA, width), F32)
    for k, value in enumerate(values):
        rest = value
        for part in range(3):
            piece = rest.astype(BF16).astype(F32)
            rest = rest - piece
            block = jnp.where(row_ids == 3 * k + part, piece, block)
    return block.astype(BF16)


def join_rows(block, count):
    wide = block.astype(F32)
    return [wide[3 * k : 3 * k + 1] + wide[3 * k + 1 : 3 * k + 2] + wide[3 * k + 2 : 3 * k + 3] for k in range(count)]


def stack_rows(values, width):
    row_ids = lax.broadcasted_iota(jnp.int32, (8, width), 0)
    block = jnp.zeros((8, width), F32)
    for k, value in enumerate(values):
        block = jnp.where(row_ids == k, value, block)
    return block


def kernel(
    xs, n, v1, v2, loss_o, g1_o, g2_o,
    raw1, raw2, n1f, n2f, own2, hop_a, hop_b, ssum, qsum, tst_s, tst_r, tr_s, tr_r,
    acc, pst, pr, gx, gfull, gother, sib_r,
    rs_s, rs_r, ti_s, ti_r, ls_s, ls_r,
    in_sem, t_sem, tst_sem, tr_sem, ag_ss, ag_rs, sb_ss, sb_rs,
    px_sem, gx_sem, sib_sem, rs_ss, rs_rs, ti_sem, ls_sem,
):
    rows, width = v1.shape
    half = n // 2
    srow = rows // STREAMS
    prow = width // xs
    part_rows = rows // n
    home = n // 4
    group_rows = float(rows * n)
    total_rows = float(rows * n * xs)
    b, f = lax.axis_index("batch"), lax.axis_index("feat")
    x, y = lax.div(b, n), lax.rem(b, n)
    z, c = lax.div(f, 2), lax.rem(f, 2)
    o = 1 - c
    is_low = c == 0
    skip = half == 4

    def dev(x_, y_, z_, c_):
        return (x_ * n + y_, z_ * 2 + c_)

    def wrap(v, m):
        return lax.rem(v + m, m)

    sibling = dev(x, y, z, o)
    partner = dev(x, z, y, c)
    x_peers = [dev(wrap(x + k, xs), y, z, c) for k in range(1, xs)]
    y_peers = [dev(x, wrap(y + k, n), z, c) for k in range(1, n)]
    z_peers = [dev(x, y, wrap(z + k, n), c) for k in range(1, n)]
    nearest = sorted(range(1, n), key=lambda k: min(k, n - k))

    def along(a, k):
        return dev(x, wrap(y + k, n), z, c) if a == 0 else dev(x, y, wrap(z + k, n), c)

    ring = [[along(a, 1), along(a, -1)] for a in range(2)]
    ring2 = [[along(a, 2), along(a, -2)] for a in range(2)] if skip else None
    pos = [y, z]
    off_diag = y != z
    on_diag = y == z
    diag_one = jnp.where(on_diag, 1.0, 0.0).astype(F32)

    def remote(src, dst, ss, rs, to):
        return pltpu.make_async_remote_copy(
            src_ref=src, dst_ref=dst, send_sem=ss, recv_sem=rs, device_id=to, device_id_type=MESH
        )

    def stream(s):
        return pl.ds(s * srow, srow)

    load1 = pltpu.make_async_copy(v1, raw1.at[c, home], in_sem.at[0])
    load2 = pltpu.make_async_copy(v2, own2, in_sem.at[1])
    load1.start()
    load2.start()
    barrier = pltpu.get_barrier_semaphore()
    greet = [sibling] + x_peers + y_peers + z_peers
    for peer in greet:
        pl.semaphore_signal(barrier, inc=1, device_id=peer, device_id_type=MESH)

    @pl.when(off_diag)
    def _():
        pl.semaphore_signal(barrier, inc=1, device_id=partner, device_id_type=MESH)

    load1.wait()
    load2.wait()

    @pl.when(off_diag)
    def _():
        pl.semaphore_wait(barrier, len(greet) + 1)

    @pl.when(on_diag)
    def _():
        pl.semaphore_wait(barrier, len(greet))

    class Swap:
        def __init__(self, src, dst, sems):
            self.far = remote(src, dst, sems.at[0], sems.at[1], partner)
            self.near = pltpu.make_async_copy(src, dst, sems.at[1])

        def start(self):
            @pl.when(off_diag)
            def _():
                self.far.start()

            @pl.when(on_diag)
            def _():
                self.near.start()

        def wait_recv(self):
            @pl.when(off_diag)
            def _():
                self.far.wait_recv()

            @pl.when(on_diag)
            def _():
                self.near.wait()

        def wait_send(self):
            @pl.when(off_diag)
            def _():
                self.far.wait_send()

    late = []

    def go(cp):
        cp.start()
        late.append(cp)

    def part(k):
        return pl.ds(pl.multiple_of(k * part_rows, part_rows), part_rows)

    class Exchange:
        def __init__(self, source, hop, target, sems, along_z):
            self.source, self.hop, self.target, self.sems = source, hop, target, sems
            self.peers = z_peers if along_z else y_peers
            self.here, self.there = (z, y) if along_z else (y, z)
            self.to = (lambda k: dev(x, k, z, c)) if along_z else (lambda k: dev(x, y, k, c))

        def first(self, k):
            return remote(
                self.source(k), self.hop.at[self.here], self.sems.at[0, k], self.sems.at[1, k], self.peers[k - 1]
            )

        def stay(self):
            return pltpu.make_async_copy(self.source(0), self.hop.at[self.here], self.sems.at[1, 0])

        def second(self, k):
            origin = wrap(self.here - k, n)
            src, sem = self.hop.at[origin], self.sems.at[3, self.there]
            far = remote(src, self.target(wrap(self.there - origin, n), origin), self.sems.at[2, k], sem, self.to(origin))
            near = pltpu.make_async_copy(src, self.target(0, self.there), sem)
            return origin, far, near

        def start(self, some):
            for k in some:
                if k == 0:
                    self.stay().start()
                else:
                    self.first(k).start()

        def pass_on(self, some):
            for k in some:
                if k == 0:
                    self.stay().wait()
                else:
                    self.first(k).wait_recv()
                origin, far, near = self.second(k)

                @pl.when(origin != self.there)
                def _():
                    far.start()

                @pl.when(origin == self.there)
                def _():
                    near.start()

        def wait_recv(self, some):
            for k in some:
                ref, sem = self.target(k, self.there), self.sems.at[3, wrap(self.there + k, n)]
                if k == 0:
                    pltpu.make_async_copy(ref, ref, sem).wait()
                else:
                    remote(ref, ref, self.sems.at[2, k], sem, self.peers[0]).wait_recv()

        def wait_send(self):
            for k in nearest:
                self.first(k).wait_send()
            for k in range(n):
                origin, far, _ = self.second(k)

                @pl.when(origin != self.there)
                def _():
                    far.wait_send()

    every_k = [0] + nearest
    spread_out = Exchange(
        lambda k: own2.at[part(wrap(z + k, n))], hop_a, lambda k, _: raw2.at[c, wrap(home + k, n), part(z)], t_sem, True
    )
    spread_out.start(every_k)

    raws, norms = (raw1, raw2), (n1f, n2f)

    def depth(d, s):
        return half if (s < STREAMS // 2) == (d == 0) else half - 1

    def ring_block(a, d, t):
        if a == 0:
            return (home + (t if d else -t)) % n
        return wrap(pos[a] - t, n) if d == 0 else wrap(pos[a] + t, n)

    def piece(a, core, block, s):
        if a == 0:
            return raw1.at[core, block, stream(s)]
        return raw2.at[core, pl.ds(s * n // STREAMS, n // STREAMS), part(block)]

    def block_of(refs, a, core, block):
        if a == 0:
            return refs[core, block]
        return refs[core, :, part(block)].reshape(rows, width)

    def ag_copy(a, d, t, s):
        far = skip and t == 3
        steps = 2 if far else t
        src = piece(a, c, ring_block(a, d, steps), s)
        dst = piece(a, c, ring_block(a, d, steps + (2 if far else 1)), s) if a == 0 else src
        return remote(src, dst, ag_ss.at[a, d, t, s], ag_rs.at[a, d, t, s], (ring2 if far else ring)[a][d])

    def sib_copy(a, core, block, s, slot):
        ref = piece(a, core, block, s)
        return remote(ref, ref, sb_ss.at[a, slot, s], sb_rs.at[a, slot, s], sibling)

    def ring_slot(d, t):
        return 1 + t if d == 0 else 1 + half + t

    def open_ring(a, s):
        for d in range(2):
            if depth(d, s) > 0:
                go(ag_copy(a, d, 0, s))
        go(sib_copy(a, c, ring_block(a, 0, 0), s, 0))

    def forward(a, t):
        for s in range(STREAMS):
            for d in range(2):
                if t >= depth(d, s):
                    continue
                ag_copy(a, d, t, s).wait_recv()
                if t + 1 < min(depth(d, s), 3 if skip else half):
                    go(ag_copy(a, d, t + 1, s))
                if skip and t == 1 and depth(d, s) == 4:
                    go(ag_copy(a, d, 3, s))
                go(sib_copy(a, c, ring_block(a, d, t + 1), s, ring_slot(d, t)))

    def sib_wait(a, s, d, t):
        if d is None:
            sib_copy(a, o, ring_block(a, 0, 0), s, 0).wait_recv()
        elif t < depth(d, s):
            sib_copy(a, o, ring_block(a, d, t + 1), s, ring_slot(d, t)).wait_recv()

    shifts = {}

    def fold(value):
        return jnp.sum(value.reshape(rows // 8, 8, width), axis=0)

    def shifted(a, block, begin):
        for h, core in enumerate((c, o)):
            value = block_of(raws[a], a, core, block).astype(F32)
            if begin:
                shifts[a, h] = jnp.sum(fold(value), axis=0, keepdims=True) / rows
            value = value - shifts[a, h]
            if a == 0:
                norms[a][core, block] = value.astype(BF16)
            else:
                norms[a][core, :, part(block)] = value.astype(BF16).reshape(n, part_rows, width)
            if begin:
                ssum[a, h] = fold(value)
                qsum[a, h] = fold(value * value)
            else:
                ssum[a, h] += fold(value)
                qsum[a, h] += fold(value * value)

    def correlate(block, begin):
        for h in range(2):
            share = lax.dot_general(
                block_of(n1f, 1, c, block), block_of(n2f, 1, h, block), (((0,), (0,)), ((), ())), preferred_element_type=F32
            )
            if begin:
                acc[h] = share
            else:
                acc[h] += share

    def blocks_of(a, t):
        if t + 1 < half:
            return [ring_block(a, 0, t + 1), ring_block(a, 1, t + 1)]
        return [ring_block(a, 0, half)]

    def arrived(a, t):
        for s in range(STREAMS):
            for d in range(2):
                sib_wait(a, s, d, t)
        for block in blocks_of(a, t):
            shifted(a, block, False)

    def correlate_all(t):
        for block in blocks_of(1, t):
            correlate(block, False)

    for s in range(STREAMS):
        open_ring(0, s)
    spread_out.pass_on(every_k)
    for s in range(STREAMS):
        spread_out.wait_recv([k for k in every_k if (home + k) % n * STREAMS // n == s])
        open_ring(1, s)
    forward(0, 0)
    for s in range(STREAMS):
        sib_wait(0, s, None, 0)
    for s in range(STREAMS):
        sib_wait(1, s, None, 0)
    shifted(0, home, True)
    shifted(1, z, True)
    for t in range(1, half):
        forward(1, t - 1)
        forward(0, t)
        arrived(0, t - 1)
        if t > 1:
            arrived(1, t - 2)
    arrived(0, half - 1)
    correlate(z, True)
    for t in range(half - 2):
        correlate_all(t)
    forward(1, half - 1)
    for t in range(max(half - 2, 0), half):
        arrived(1, t)
        correlate_all(t)

    def spread(row, count, first):
        ids = lax.broadcasted_iota(jnp.int32, (count, width), 0) + first
        lanes = lax.broadcasted_iota(jnp.int32, (count, width), 1)
        return jnp.sum(jnp.where(ids == lanes, row, 0.0), axis=1, keepdims=True)

    rests, means, squares = {}, {}, {}
    for a in range(2):
        for h in range(2):
            rest = jnp.sum(ssum[a, h], axis=0, keepdims=True) / group_rows
            rests[a, h] = rest
            means[a, h] = shifts[a, h] + rest
            squares[a, h] = jnp.sum(qsum[a, h], axis=0, keepdims=True) - group_rows * rest * rest

    def by_half(table, a):
        return [jnp.where(is_low, table[a, 0], table[a, 1]), jnp.where(is_low, table[a, 1], table[a, 0])]

    rest2, mean2, square2 = by_half(rests, 1), by_half(means, 1), by_half(squares, 1)
    column = spread(rests[0, 0], width, 0) * (group_rows / total_rows)
    row_ids = lax.broadcasted_iota(jnp.int32, (width, width), 0)
    col_ids = lax.broadcasted_iota(jnp.int32, (width, width), 1)
    for h in range(2):
        acc[h] = acc[h] / total_rows - column * rest2[h]
    diag = jnp.sum(jnp.where(row_ids == col_ids, acc[c], 0.0), axis=0, keepdims=True) * diag_one
    facts = [
        [means[0, 0], squares[0, 0], mean2[0], square2[0], diag],
        [means[0, 1], squares[0, 1], mean2[1], square2[1]],
    ]

    for h in range(2):
        extra = split_rows(facts[h], width)
        for k in range(xs):
            pst[k, h, :prow] = acc[h, k * prow : (k + 1) * prow].astype(BF16)
            pst[k, h, prow:] = extra
    px = [
        remote(pst.at[wrap(x + k, xs)], pr.at[k - 1], px_sem.at[0, k - 1], px_sem.at[1, k - 1], x_peers[k - 1])
        for k in range(1, xs)
    ]
    for cp in px:
        go(cp)
    for cp in px:
        cp.wait_recv()
    every = [facts]
    for k in range(xs - 1):
        every.append([join_rows(pr[k, 0, prow:], 5), join_rows(pr[k, 1, prow:], 4)])

    def whole(h, place):
        center = sum(e[h][place] for e in every) / xs
        spreads = [e[h][place] - center for e in every]
        square = sum(e[h][place + 1] for e in every) + group_rows * sum(v * v for v in spreads)
        return center, 1.0 / jnp.sqrt(square / total_rows + EPSILON), spreads

    center1, inv1, spread1 = whole(0, 0)
    center1o, inv1o, _ = whole(1, 0)
    center2, inv2, spread2 = [[v[h] for h in range(2)] for v in zip(*[whole(h, 2) for h in range(2)])]
    near2 = [jnp.where(is_low, v[0], v[1]) for v in (center2, inv2)]
    near_spread2 = [jnp.where(is_low, u, w) for u, w in zip(*spread2)]
    tst_s[...] = stack_rows(near2, width)
    swap_st = Swap(tst_s, tst_r, tst_sem)
    swap_st.start()

    diag = sum(e[0][4] for e in every) + sum(u * w for u, w in zip(spread1, near_spread2)) / xs * diag_one
    diag = diag * inv1 * near2[1]
    diag_grad = (-2.0 * (1.0 - diag)).astype(BF16).astype(F32) * diag_one
    prow_ids = lax.broadcasted_iota(jnp.int32, (prow, width), 0) + x * prow
    pcol_ids = lax.broadcasted_iota(jnp.int32, (prow, width), 1)
    same = prow_ids == pcol_ids
    inv_column = spread(inv1, prow, x * prow)
    spread_columns = [spread(v, prow, x * prow) / xs for v in spread1]
    loss = jnp.zeros((1, 1), F32)
    row_trace = jnp.zeros((prow, 1), F32)
    col_trace = []
    for h in range(2):
        corr = acc[h, pl.ds(pl.multiple_of(x * prow, prow), prow)]
        for k in range(xs - 1):
            corr = corr + pr[k, h, :prow].astype(F32)
        for k in range(xs):
            corr = corr + spread_columns[k] * spread2[h][k]
        corr = corr * inv_column * inv2[h]
        spot = same & on_diag & (c == h)
        terms = jnp.where(spot, (1.0 - diag) * (1.0 - diag), OFF_WEIGHT * corr * corr)
        loss = loss + jnp.sum(jnp.sum(terms, axis=0, keepdims=True), axis=1, keepdims=True)
        grad = jnp.where(spot, 0.0, 2.0 * OFF_WEIGHT * corr).astype(BF16)
        gx[x, h, :prow] = grad
        share = corr * grad.astype(F32)
        row_trace = row_trace + jnp.sum(share, axis=1, keepdims=True)
        col_trace.append(jnp.sum(share, axis=0, keepdims=True))
    row_trace = jnp.sum(jnp.where(same, row_trace, 0.0), axis=0, keepdims=True)
    loss_row = jnp.zeros((1, width), F32) + loss
    gx[x, 0, prow:] = split_rows([col_trace[0], row_trace, loss_row], width)
    gx[x, 1, prow:] = split_rows([col_trace[1], row_trace, loss_row], width)
    gc = [remote(gx.at[x], gx.at[x], gx_sem.at[0, k], gx_sem.at[1, k], to) for k, to in enumerate(x_peers)]
    for cp in gc:
        cp.start()

    def over(k):
        return remote(gx.at[k, o], sib_r.at[k], sib_sem.at[0, k], sib_sem.at[1, k], sibling)

    over(x).start()

    def standard(i, _):
        n1f[c, i] = ((raw1[c, i].astype(F32) - center1) * inv1).astype(BF16)
        n1f[o, i] = ((raw1[o, i].astype(F32) - center1o) * inv1o).astype(BF16)
        for h in range(2):
            n2f[h, i] = ((raw2[h, i].astype(F32) - center2[h]) * inv2[h]).astype(BF16)
        return 0

    lax.fori_loop(0, n, standard, 0)
    for cp in late:
        cp.wait_send()
    spread_out.wait_send()
    swap_st.wait_send()
    for k in range(1, xs):
        src = wrap(x - k, xs)
        remote(gx.at[src], gx.at[src], gx_sem.at[0, k - 1], gx_sem.at[1, k - 1], x_peers[k - 1]).wait_recv()
        over(src).start()
    col0 = col1 = trace1 = loss_row = jnp.zeros((1, width), F32)
    for k in range(xs):
        for h in range(2):
            gfull[h, k * prow : (k + 1) * prow] = gx[k, h, :prow]
        got = join_rows(gx[k, 0, prow:], 3)
        col0, trace1, loss_row = col0 + got[0], trace1 + got[1], loss_row + got[2]
        col1 = col1 + join_rows(gx[k, 1, prow:], 1)[0]
    diag_trace = diag * diag_grad
    trace1 = trace1 + diag_trace
    trace2 = jnp.where(is_low, col0, col1) + diag_trace
    late = gc
    for k in range(xs):
        over(k).wait_recv()
    for k in range(xs):
        gother[k * prow : (k + 1) * prow] = sib_r[k, :prow]
        got = join_rows(sib_r[k, prow:], 3)
        trace2 = trace2 + got[0]
        loss_row = loss_row + got[2]

    ring_extra = [[trace1, diag_grad], [trace2, loss_row]]

    def product(a, block, s):
        if a == 0:
            dims = (((1,), (1,)), ((), ()))
            left, right = [n2f[h, block, stream(s)] for h in range(2)], (gfull[0], gfull[1])
        else:
            dims = (((1,), (0,)), ((), ()))
            images = pl.ds(s * n // STREAMS, n // STREAMS)
            left = [n1f[h, images, part(block)].reshape(srow, width) for h in (c, o)]
            right = (gfull[c], gother[...])
        return lax.dot_general(left[0], right[0], dims, preferred_element_type=F32) + lax.dot_general(
            left[1], right[1], dims, preferred_element_type=F32
        )

    def rs_copy(a, d, t, s):
        far = skip and t == 0 and depth(d, s) == 4
        sub = pl.ds(0, srow + (EXTRA if s == 0 else 0))
        return remote(
            rs_s.at[a, d, t, s, sub], rs_r.at[a, d, t, s, sub], rs_ss.at[a, d, t, s], rs_rs.at[a, d, t, s],
            (ring2 if far else ring)[a][d],
        )

    def takes(d, t, s):
        if skip and depth(d, s) == 4:
            return {0: [], 1: [], 2: [0, 1], 3: [2]}[t]
        return [t - 1] if t > 0 else []

    def add_in(a, d, s, value, carried, messages):
        for m in messages:
            rs_copy(a, d, m, s).wait_recv()
            value = value + rs_r[a, d, m, s, :srow].astype(F32)
            if s == 0:
                got = join_rows(rs_r[a, d, m, s, srow:], 2)
                carried = [u + w for u, w in zip(carried, got)]
        return value, carried

    def rs_send(a, d, t, s):
        block = ring_block(a, 1 - d, depth(d, s) - t)
        value, carried = add_in(a, d, s, product(a, block, s), ring_extra[a], takes(d, t, s))
        rs_s[a, d, t, s, :srow] = value.astype(BF16)
        if s == 0:
            rs_s[a, d, t, s, srow:] = split_rows(carried, width)
        go(rs_copy(a, d, t, s))

    lanes = [(s, a, d) for s in reversed(range(STREAMS)) for a in (1, 0) for d in range(2)]
    for step in range(half):
        for s, a, d in lanes:
            deep = depth(d, s)
            if skip and deep == 4:
                for t in ([0, 1], [2], [3], [])[step]:
                    rs_send(a, d, t, s)
            elif step < deep:
                rs_send(a, d, step, s)

    def finish(a, s):
        value, carried = product(a, ring_block(a, 0, 0), s), ring_extra[a]
        for d in range(2):
            if depth(d, s) > 0:
                value, carried = add_in(a, d, s, value, carried, [depth(d, s) - 1])
        return value, carried

    come_back = Exchange(
        lambda k: ti_s.at[(home + k) % n], hop_b, lambda k, base: ti_r.at[part(wrap(base + k, n))], ti_sem, False
    )
    for s in reversed(range(STREAMS)):
        value, carried = finish(1, s)
        ti_s[pl.ds(s * n // STREAMS, n // STREAMS)] = value.astype(BF16).reshape(n // STREAMS, part_rows, width)
        if s == 0:
            trace2, loss_row = carried
        come_back.start([k for k in reversed(every_k) if (home + k) % n * STREAMS // n == s])
    tr_s[...] = stack_rows([trace2], width)
    swap_tr = Swap(tr_s, tr_r, tr_sem)
    swap_tr.start()
    swap_st.wait_recv()
    far_center, far_inv = tst_r[0:1], tst_r[1:2]
    second = ((own2[...].astype(F32) - far_center) * far_inv).astype(BF16)
    own2[...] = second
    come_back.pass_on(every_k)
    ls_s[...] = jnp.zeros((8, width), F32) + loss_row
    lc = [remote(ls_s, ls_r.at[k], ls_sem.at[0, k], ls_sem.at[1, k], to) for k, to in enumerate(y_peers)]
    for cp in lc:
        go(cp)
    for s in range(STREAMS):
        value, carried = finish(0, s)
        if s == 0:
            trace1, diag_grad = carried
        value = value + own2[stream(s)].astype(F32) * diag_grad - n1f[c, home, stream(s)].astype(F32) * trace1
        g1_o[stream(s)] = (LOSS_SCALE * value * inv1).astype(BF16)
    for cp in late:
        cp.wait_send()
    for k in range(xs):
        over(k).wait_send()
    for cp in lc:
        cp.wait_recv()
    for k in range(n - 1):
        loss_row = loss_row + ls_r[k, 0:1]
    loss_o[...] = loss_row[:, 0:1]
    swap_tr.wait_recv()
    trace2 = tr_r[0:1]
    come_back.wait_recv(every_k)
    value = ti_r[...].astype(F32) + n1f[c, home].astype(F32) * diag_grad - own2[...].astype(F32) * trace2
    g2_o[...] = (LOSS_SCALE * value * far_inv).astype(BF16)
    come_back.wait_send()
    swap_tr.wait_send()


def on_device(xs, n, view_one, view_two):
    rows, width = view_one.shape
    half = n // 2
    srow = rows // STREAMS
    prow = width // xs
    sem = pltpu.SemaphoreType.DMA
    blocks = (2, n, rows, width)
    ring = (2, 2, half, STREAMS)
    loss, grad_one, grad_two = pl.pallas_call(
        functools.partial(kernel, xs, n),
        out_shape=(
            jax.ShapeDtypeStruct((1, 1), F32),
            jax.ShapeDtypeStruct((rows, width), BF16),
            jax.ShapeDtypeStruct((rows, width), BF16),
        ),
        in_specs=[pl.BlockSpec(memory_space=pltpu.HBM)] * 2,
        out_specs=[pl.BlockSpec(memory_space=pltpu.VMEM)] * 3,
        scratch_shapes=[
            pltpu.VMEM(blocks, BF16),
            pltpu.VMEM(blocks, BF16),
            pltpu.VMEM(blocks, BF16),
            pltpu.VMEM(blocks, BF16),
            pltpu.VMEM((rows, width), BF16),
            pltpu.VMEM((n, rows // n, width), BF16),
            pltpu.VMEM((n, rows // n, width), BF16),
            pltpu.VMEM((2, 2, 8, width), F32),
            pltpu.VMEM((2, 2, 8, width), F32),
            pltpu.VMEM((8, width), F32),
            pltpu.VMEM((8, width), F32),
            pltpu.VMEM((8, width), F32),
            pltpu.VMEM((8, width), F32),
            pltpu.VMEM((2, width, width), F32),
            pltpu.VMEM((xs, 2, prow + EXTRA, width), BF16),
            pltpu.VMEM((xs - 1, 2, prow + EXTRA, width), BF16),
            pltpu.VMEM((xs, 2, prow + EXTRA, width), BF16),
            pltpu.VMEM((2, width, width), BF16),
            pltpu.VMEM((width, width), BF16),
            pltpu.VMEM((xs, prow + EXTRA, width), BF16),
            pltpu.VMEM(ring + (srow + EXTRA, width), BF16),
            pltpu.VMEM(ring + (srow + EXTRA, width), BF16),
            pltpu.VMEM((n, rows // n, width), BF16),
            pltpu.VMEM((rows, width), BF16),
            pltpu.VMEM((8, width), F32),
            pltpu.VMEM((n - 1, 8, width), F32),
            sem((2,)),
            sem((4, n)),
            sem((2,)),
            sem((2,)),
            sem(ring),
            sem(ring),
            sem((2, n + 1, STREAMS)),
            sem((2, n + 1, STREAMS)),
            sem((2, xs - 1)),
            sem((2, xs - 1)),
            sem((2, xs)),
            sem(ring),
            sem(ring),
            sem((4, n)),
            sem((2, n - 1)),
        ],
        compiler_params=pltpu.CompilerParams(
            collective_id=0, has_side_effects=True, vmem_limit_bytes=60 * 2**20
        ),
        name="barlow",
    )(view_one, view_two)
    return loss.reshape(()), grad_one, grad_two


def solution(mesh):
    n = mesh.shape["feat"] // 2
    xs = mesh.shape["batch"] // n
    spec = P("batch", "feat")
    return jax.shard_map(
        functools.partial(on_device, xs, n),
        mesh=mesh,
        in_specs=(spec, spec),
        out_specs=(P(), spec, spec),
        check_vma=False,
    )
```

```python
import functools

import jax
import jax.numpy as jnp
from jax import lax
from jax.experimental import pallas as pl
from jax.experimental.pallas import tpu as pltpu
from jax.sharding import PartitionSpec as P

OFF_WEIGHT = 0.0051
EPSILON = 1e-05
LOSS_SCALE = 16.0
MESH = pl.DeviceIdType.MESH
F32 = jnp.float32
BF16 = jnp.bfloat16
STREAMS = 2
EXTRA = 16


def split_rows(values, width):
    row_ids = lax.broadcasted_iota(jnp.int32, (EXTRA, width), 0)
    block = jnp.zeros((EXTRA, width), F32)
    for k, value in enumerate(values):
        rest = value
        for part in range(3):
            piece = rest.astype(BF16).astype(F32)
            rest = rest - piece
            block = jnp.where(row_ids == 3 * k + part, piece, block)
    return block.astype(BF16)


def join_rows(block, count):
    wide = block.astype(F32)
    return [wide[3 * k : 3 * k + 1] + wide[3 * k + 1 : 3 * k + 2] + wide[3 * k + 2 : 3 * k + 3] for k in range(count)]


def stack_rows(values, width):
    row_ids = lax.broadcasted_iota(jnp.int32, (8, width), 0)
    block = jnp.zeros((8, width), F32)
    for k, value in enumerate(values):
        block = jnp.where(row_ids == k, value, block)
    return block


def kernel(
    xs, n, v1, v2, loss_o, g1_o, g2_o,
    raw1, raw2, n1f, n2f, own2, hop_a, hop_b, ssum, qsum, tst_s, tst_r, tr_s, tr_r,
    acc, pst, pr, gx, gfull, gother, sib_r,
    rs_s, rs_r, ti_s, ti_r, ls_s, ls_r,
    in_sem, t_sem, tst_sem, tr_sem, ag_ss, ag_rs, sb_ss, sb_rs,
    px_sem, gx_sem, sib_sem, rs_ss, rs_rs, ti_sem, ls_sem,
):
    rows, width = v1.shape
    half = n // 2
    srow = rows // STREAMS
    prow = width // xs
    part_rows = rows // n
    home = n // 4
    group_rows = float(rows * n)
    total_rows = float(rows * n * xs)
    b, f = lax.axis_index("batch"), lax.axis_index("feat")
    x, y = lax.div(b, n), lax.rem(b, n)
    z, c = lax.div(f, 2), lax.rem(f, 2)
    o = 1 - c
    is_low = c == 0
    skip = half == 4

    def dev(x_, y_, z_, c_):
        return (x_ * n + y_, z_ * 2 + c_)

    def wrap(v, m):
        return lax.rem(v + m, m)

    sibling = dev(x, y, z, o)
    partner = dev(x, z, y, c)
    x_peers = [dev(wrap(x + k, xs), y, z, c) for k in range(1, xs)]
    y_peers = [dev(x, wrap(y + k, n), z, c) for k in range(1, n)]
    z_peers = [dev(x, y, wrap(z + k, n), c) for k in range(1, n)]
    nearest = sorted(range(1, n), key=lambda k: min(k, n - k))

    def along(a, k):
        return dev(x, wrap(y + k, n), z, c) if a == 0 else dev(x, y, wrap(z + k, n), c)

    ring = [[along(a, 1), along(a, -1)] for a in range(2)]
    ring2 = [[along(a, 2), along(a, -2)] for a in range(2)] if skip else None
    pos = [y, z]
    off_diag = y != z
    on_diag = y == z
    diag_one = jnp.where(on_diag, 1.0, 0.0).astype(F32)

    def remote(src, dst, ss, rs, to):
        return pltpu.make_async_remote_copy(
            src_ref=src, dst_ref=dst, send_sem=ss, recv_sem=rs, device_id=to, device_id_type=MESH
        )

    def stream(s):
        return pl.ds(s * srow, srow)

    load1 = pltpu.make_async_copy(v1, raw1.at[c, home], in_sem.at[0])
    load2 = pltpu.make_async_copy(v2, own2, in_sem.at[1])
    load1.start()
    load2.start()
    barrier = pltpu.get_barrier_semaphore()
    greet = [sibling] + x_peers + y_peers + z_peers
    for peer in greet:
        pl.semaphore_signal(barrier, inc=1, device_id=peer, device_id_type=MESH)

    @pl.when(off_diag)
    def _():
        pl.semaphore_signal(barrier, inc=1, device_id=partner, device_id_type=MESH)

    load1.wait()
    load2.wait()

    @pl.when(off_diag)
    def _():
        pl.semaphore_wait(barrier, len(greet) + 1)

    @pl.when(on_diag)
    def _():
        pl.semaphore_wait(barrier, len(greet))

    class Swap:
        def __init__(self, src, dst, sems):
            self.far = remote(src, dst, sems.at[0], sems.at[1], partner)
            self.near = pltpu.make_async_copy(src, dst, sems.at[1])

        def start(self):
            @pl.when(off_diag)
            def _():
                self.far.start()

            @pl.when(on_diag)
            def _():
                self.near.start()

        def wait_recv(self):
            @pl.when(off_diag)
            def _():
                self.far.wait_recv()

            @pl.when(on_diag)
            def _():
                self.near.wait()

        def wait_send(self):
            @pl.when(off_diag)
            def _():
                self.far.wait_send()

    late = []

    def go(cp):
        cp.start()
        late.append(cp)

    def part(k):
        return pl.ds(pl.multiple_of(k * part_rows, part_rows), part_rows)

    class Exchange:
        def __init__(self, source, hop, target, sems, along_z):
            self.source, self.hop, self.target, self.sems = source, hop, target, sems
            self.peers = z_peers if along_z else y_peers
            self.here, self.there = (z, y) if along_z else (y, z)
            self.to = (lambda k: dev(x, k, z, c)) if along_z else (lambda k: dev(x, y, k, c))

        def first(self, k):
            return remote(
                self.source(k), self.hop.at[self.here], self.sems.at[0, k], self.sems.at[1, k], self.peers[k - 1]
            )

        def stay(self):
            return pltpu.make_async_copy(self.source(0), self.hop.at[self.here], self.sems.at[1, 0])

        def second(self, k):
            origin = wrap(self.here - k, n)
            src, sem = self.hop.at[origin], self.sems.at[3, self.there]
            far = remote(src, self.target(wrap(self.there - origin, n), origin), self.sems.at[2, k], sem, self.to(origin))
            near = pltpu.make_async_copy(src, self.target(0, self.there), sem)
            return origin, far, near

        def start(self, some):
            for k in some:
                if k == 0:
                    self.stay().start()
                else:
                    self.first(k).start()

        def pass_on(self, some):
            for k in some:
                if k == 0:
                    self.stay().wait()
                else:
                    self.first(k).wait_recv()
                origin, far, near = self.second(k)

                @pl.when(origin != self.there)
                def _():
                    far.start()

                @pl.when(origin == self.there)
                def _():
                    near.start()

        def wait_recv(self, some):
            for k in some:
                ref, sem = self.target(k, self.there), self.sems.at[3, wrap(self.there + k, n)]
                if k == 0:
                    pltpu.make_async_copy(ref, ref, sem).wait()
                else:
                    remote(ref, ref, self.sems.at[2, k], sem, self.peers[0]).wait_recv()

        def wait_send(self):
            for k in nearest:
                self.first(k).wait_send()
            for k in range(n):
                origin, far, _ = self.second(k)

                @pl.when(origin != self.there)
                def _():
                    far.wait_send()

    every_k = [0] + nearest
    spread_out = Exchange(
        lambda k: own2.at[part(wrap(z + k, n))], hop_a, lambda k, _: raw2.at[c, wrap(home + k, n), part(z)], t_sem, True
    )
    spread_out.start(every_k[::-1])

    raws, norms = (raw1, raw2), (n1f, n2f)

    def depth(d, s):
        return half if (s < STREAMS // 2) == (d == 0) else half - 1

    def ring_block(a, d, t):
        if a == 0:
            return (home + (t if d else -t)) % n
        return wrap(pos[a] - t, n) if d == 0 else wrap(pos[a] + t, n)

    def piece(a, core, block, s):
        if a == 0:
            return raw1.at[core, block, stream(s)]
        return raw2.at[core, pl.ds(s * n // STREAMS, n // STREAMS), part(block)]

    def block_of(refs, a, core, block):
        if a == 0:
            return refs[core, block]
        return refs[core, :, part(block)].reshape(rows, width)

    def ag_copy(a, d, t, s):
        far = skip and t == 3
        steps = 2 if far else t
        src = piece(a, c, ring_block(a, d, steps), s)
        dst = piece(a, c, ring_block(a, d, steps + (2 if far else 1)), s) if a == 0 else src
        return remote(src, dst, ag_ss.at[a, d, t, s], ag_rs.at[a, d, t, s], (ring2 if far else ring)[a][d])

    def sib_copy(a, core, block, s, slot):
        ref = piece(a, core, block, s)
        return remote(ref, ref, sb_ss.at[a, slot, s], sb_rs.at[a, slot, s], sibling)

    def ring_slot(d, t):
        return 1 + t if d == 0 else 1 + half + t

    def open_ring(a, s):
        for d in range(2):
            if depth(d, s) > 0:
                go(ag_copy(a, d, 0, s))
        go(sib_copy(a, c, ring_block(a, 0, 0), s, 0))

    def forward(a, t):
        for s in range(STREAMS):
            for d in range(2):
                if t >= depth(d, s):
                    continue
                ag_copy(a, d, t, s).wait_recv()
                if t + 1 < min(depth(d, s), 3 if skip else half):
                    go(ag_copy(a, d, t + 1, s))
                if skip and t == 1 and depth(d, s) == 4:
                    go(ag_copy(a, d, 3, s))
                go(sib_copy(a, c, ring_block(a, d, t + 1), s, ring_slot(d, t)))

    def sib_wait(a, s, d, t):
        if d is None:
            sib_copy(a, o, ring_block(a, 0, 0), s, 0).wait_recv()
        elif t < depth(d, s):
            sib_copy(a, o, ring_block(a, d, t + 1), s, ring_slot(d, t)).wait_recv()

    shifts = {}

    def fold(value):
        return jnp.sum(value.reshape(rows // 8, 8, width), axis=0)

    def shifted(a, block, begin):
        for h, core in enumerate((c, o)):
            value = block_of(raws[a], a, core, block).astype(F32)
            if begin:
                shifts[a, h] = jnp.sum(fold(value), axis=0, keepdims=True) / rows
            value = value - shifts[a, h]
            if a == 0:
                norms[a][core, block] = value.astype(BF16)
            else:
                norms[a][core, :, part(block)] = value.astype(BF16).reshape(n, part_rows, width)
            if begin:
                ssum[a, h] = fold(value)
                qsum[a, h] = fold(value * value)
            else:
                ssum[a, h] += fold(value)
                qsum[a, h] += fold(value * value)

    def correlate(block, begin):
        for h in range(2):
            share = lax.dot_general(
                block_of(n1f, 1, c, block), block_of(n2f, 1, h, block), (((0,), (0,)), ((), ())), preferred_element_type=F32
            )
            if begin:
                acc[h] = share
            else:
                acc[h] += share

    def blocks_of(a, t):
        if t + 1 < half:
            return [ring_block(a, 0, t + 1), ring_block(a, 1, t + 1)]
        return [ring_block(a, 0, half)]

    def arrived(a, t):
        for s in range(STREAMS):
            for d in range(2):
                sib_wait(a, s, d, t)
        for block in blocks_of(a, t):
            shifted(a, block, False)

    def correlate_all(t):
        for block in blocks_of(1, t):
            correlate(block, False)

    for s in range(STREAMS):
        open_ring(0, s)
    spread_out.pass_on(every_k)
    for s in range(STREAMS):
        spread_out.wait_recv([k for k in every_k if (home + k) % n * STREAMS // n == s])
        open_ring(1, s)
    forward(0, 0)
    for s in range(STREAMS):
        sib_wait(0, s, None, 0)
    for s in range(STREAMS):
        sib_wait(1, s, None, 0)
    shifted(0, home, True)
    shifted(1, z, True)
    for t in range(1, half):
        forward(1, t - 1)
        forward(0, t)
        arrived(0, t - 1)
        if t > 1:
            arrived(1, t - 2)
    arrived(0, half - 1)
    correlate(z, True)
    for t in range(half - 2):
        correlate_all(t)
    forward(1, half - 1)
    for t in range(max(half - 2, 0), half):
        arrived(1, t)
        correlate_all(t)

    def spread(row, count, first):
        ids = lax.broadcasted_iota(jnp.int32, (count, width), 0) + first
        lanes = lax.broadcasted_iota(jnp.int32, (count, width), 1)
        return jnp.sum(jnp.where(ids == lanes, row, 0.0), axis=1, keepdims=True)

    rests, means, squares = {}, {}, {}
    for a in range(2):
        for h in range(2):
            rest = jnp.sum(ssum[a, h], axis=0, keepdims=True) / group_rows
            rests[a, h] = rest
            means[a, h] = shifts[a, h] + rest
            squares[a, h] = jnp.sum(qsum[a, h], axis=0, keepdims=True) - group_rows * rest * rest

    def by_half(table, a):
        return [jnp.where(is_low, table[a, 0], table[a, 1]), jnp.where(is_low, table[a, 1], table[a, 0])]

    rest2, mean2, square2 = by_half(rests, 1), by_half(means, 1), by_half(squares, 1)
    column = spread(rests[0, 0], width, 0) * (group_rows / total_rows)
    row_ids = lax.broadcasted_iota(jnp.int32, (width, width), 0)
    col_ids = lax.broadcasted_iota(jnp.int32, (width, width), 1)
    for h in range(2):
        acc[h] = acc[h] / total_rows - column * rest2[h]
    diag = jnp.sum(jnp.where(row_ids == col_ids, acc[c], 0.0), axis=0, keepdims=True) * diag_one
    facts = [
        [means[0, 0], squares[0, 0], mean2[0], square2[0], diag],
        [means[0, 1], squares[0, 1], mean2[1], square2[1]],
    ]

    for h in range(2):
        extra = split_rows(facts[h], width)
        for k in range(xs):
            pst[k, h, :prow] = acc[h, k * prow : (k + 1) * prow].astype(BF16)
            pst[k, h, prow:] = extra
    px = [
        remote(pst.at[wrap(x + k, xs)], pr.at[k - 1], px_sem.at[0, k - 1], px_sem.at[1, k - 1], x_peers[k - 1])
        for k in range(1, xs)
    ]
    for cp in px[1:2] + px[:1] + px[2:]:
        go(cp)
    for cp in px:
        cp.wait_recv()
    every = [facts]
    for k in range(xs - 1):
        every.append([join_rows(pr[k, 0, prow:], 5), join_rows(pr[k, 1, prow:], 4)])

    def whole(h, place):
        center = sum(e[h][place] for e in every) / xs
        spreads = [e[h][place] - center for e in every]
        square = sum(e[h][place + 1] for e in every) + group_rows * sum(v * v for v in spreads)
        return center, 1.0 / jnp.sqrt(square / total_rows + EPSILON), spreads

    center1, inv1, spread1 = whole(0, 0)
    center1o, inv1o, _ = whole(1, 0)
    center2, inv2, spread2 = [[v[h] for h in range(2)] for v in zip(*[whole(h, 2) for h in range(2)])]
    near2 = [jnp.where(is_low, v[0], v[1]) for v in (center2, inv2)]
    near_spread2 = [jnp.where(is_low, u, w) for u, w in zip(*spread2)]
    tst_s[...] = stack_rows(near2, width)
    swap_st = Swap(tst_s, tst_r, tst_sem)
    swap_st.start()

    diag = sum(e[0][4] for e in every) + sum(u * w for u, w in zip(spread1, near_spread2)) / xs * diag_one
    diag = diag * inv1 * near2[1]
    diag_grad = (-2.0 * (1.0 - diag)).astype(BF16).astype(F32) * diag_one
    prow_ids = lax.broadcasted_iota(jnp.int32, (prow, width), 0) + x * prow
    pcol_ids = lax.broadcasted_iota(jnp.int32, (prow, width), 1)
    same = prow_ids == pcol_ids
    inv_column = spread(inv1, prow, x * prow)
    spread_columns = [spread(v, prow, x * prow) / xs for v in spread1]
    loss = jnp.zeros((1, 1), F32)
    row_trace = jnp.zeros((prow, 1), F32)
    col_trace = []
    for h in range(2):
        corr = acc[h, pl.ds(pl.multiple_of(x * prow, prow), prow)]
        for k in range(xs - 1):
            corr = corr + pr[k, h, :prow].astype(F32)
        for k in range(xs):
            corr = corr + spread_columns[k] * spread2[h][k]
        corr = corr * inv_column * inv2[h]
        spot = same & on_diag & (c == h)
        terms = jnp.where(spot, (1.0 - diag) * (1.0 - diag), OFF_WEIGHT * corr * corr)
        loss = loss + jnp.sum(jnp.sum(terms, axis=0, keepdims=True), axis=1, keepdims=True)
        grad = jnp.where(spot, 0.0, 2.0 * OFF_WEIGHT * corr).astype(BF16)
        gx[x, h, :prow] = grad
        share = corr * grad.astype(F32)
        row_trace = row_trace + jnp.sum(share, axis=1, keepdims=True)
        col_trace.append(jnp.sum(share, axis=0, keepdims=True))
    row_trace = jnp.sum(jnp.where(same, row_trace, 0.0), axis=0, keepdims=True)
    loss_row = jnp.zeros((1, width), F32) + loss
    gx[x, 0, prow:] = split_rows([col_trace[0], row_trace, loss_row], width)
    gx[x, 1, prow:] = split_rows([col_trace[1], row_trace, loss_row], width)
    gc = [remote(gx.at[x], gx.at[x], gx_sem.at[0, k], gx_sem.at[1, k], to) for k, to in enumerate(x_peers)]
    for cp in gc[1:2] + gc[:1] + gc[2:]:
        cp.start()

    def over(k):
        return remote(gx.at[k, o], sib_r.at[k], sib_sem.at[0, k], sib_sem.at[1, k], sibling)

    over(x).start()

    def standard(i, _):
        n1f[c, i] = ((raw1[c, i].astype(F32) - center1) * inv1).astype(BF16)
        n1f[o, i] = ((raw1[o, i].astype(F32) - center1o) * inv1o).astype(BF16)
        for h in range(2):
            n2f[h, i] = ((raw2[h, i].astype(F32) - center2[h]) * inv2[h]).astype(BF16)
        return 0

    lax.fori_loop(0, n, standard, 0)
    for cp in late:
        cp.wait_send()
    spread_out.wait_send()
    swap_st.wait_send()
    for k in range(1, xs):
        src = wrap(x - k, xs)
        remote(gx.at[src], gx.at[src], gx_sem.at[0, k - 1], gx_sem.at[1, k - 1], x_peers[k - 1]).wait_recv()
        over(src).start()
    col0 = col1 = trace1 = loss_row = jnp.zeros((1, width), F32)
    for k in range(xs):
        for h in range(2):
            gfull[h, k * prow : (k + 1) * prow] = gx[k, h, :prow]
        got = join_rows(gx[k, 0, prow:], 3)
        col0, trace1, loss_row = col0 + got[0], trace1 + got[1], loss_row + got[2]
        col1 = col1 + join_rows(gx[k, 1, prow:], 1)[0]
    diag_trace = diag * diag_grad
    trace1 = trace1 + diag_trace
    trace2 = jnp.where(is_low, col0, col1) + diag_trace
    late = gc
    for k in range(xs):
        over(k).wait_recv()
    for k in range(xs):
        gother[k * prow : (k + 1) * prow] = sib_r[k, :prow]
        got = join_rows(sib_r[k, prow:], 3)
        trace2 = trace2 + got[0]
        loss_row = loss_row + got[2]

    ring_extra = [[trace1, diag_grad], [trace2, loss_row]]

    def product(a, block, s):
        if a == 0:
            dims = (((1,), (1,)), ((), ()))
            left, right = [n2f[h, block, stream(s)] for h in range(2)], (gfull[0], gfull[1])
        else:
            dims = (((1,), (0,)), ((), ()))
            images = pl.ds(s * n // STREAMS, n // STREAMS)
            left = [n1f[h, images, part(block)].reshape(srow, width) for h in (c, o)]
            right = (gfull[c], gother[...])
        return lax.dot_general(left[0], right[0], dims, preferred_element_type=F32) + lax.dot_general(
            left[1], right[1], dims, preferred_element_type=F32
        )

    def rs_copy(a, d, t, s):
        far = skip and t == 0 and depth(d, s) == 4
        sub = pl.ds(0, srow + (EXTRA if s == 0 else 0))
        return remote(
            rs_s.at[a, d, t, s, sub], rs_r.at[a, d, t, s, sub], rs_ss.at[a, d, t, s], rs_rs.at[a, d, t, s],
            (ring2 if far else ring)[a][d],
        )

    def takes(d, t, s):
        if skip and depth(d, s) == 4:
            return {0: [], 1: [], 2: [0, 1], 3: [2]}[t]
        return [t - 1] if t > 0 else []

    def add_in(a, d, s, value, carried, messages):
        for m in messages:
            rs_copy(a, d, m, s).wait_recv()
            value = value + rs_r[a, d, m, s, :srow].astype(F32)
            if s == 0:
                got = join_rows(rs_r[a, d, m, s, srow:], 2)
                carried = [u + w for u, w in zip(carried, got)]
        return value, carried

    def rs_send(a, d, t, s):
        block = ring_block(a, 1 - d, depth(d, s) - t)
        value, carried = add_in(a, d, s, product(a, block, s), ring_extra[a], takes(d, t, s))
        rs_s[a, d, t, s, :srow] = value.astype(BF16)
        if s == 0:
            rs_s[a, d, t, s, srow:] = split_rows(carried, width)
        go(rs_copy(a, d, t, s))

    lanes = [(s, a, d) for s in reversed(range(STREAMS)) for a in (1, 0) for d in range(2)]
    for step in range(half):
        for s, a, d in lanes:
            deep = depth(d, s)
            if skip and deep == 4:
                for t in ([0, 1], [2], [3], [])[step]:
                    rs_send(a, d, t, s)
            elif step < deep:
                rs_send(a, d, step, s)

    def finish(a, s):
        value, carried = product(a, ring_block(a, 0, 0), s), ring_extra[a]
        for d in range(2):
            if depth(d, s) > 0:
                value, carried = add_in(a, d, s, value, carried, [depth(d, s) - 1])
        return value, carried

    come_back = Exchange(
        lambda k: ti_s.at[(home + k) % n], hop_b, lambda k, base: ti_r.at[part(wrap(base + k, n))], ti_sem, False
    )
    for s in reversed(range(STREAMS)):
        value, carried = finish(1, s)
        ti_s[pl.ds(s * n // STREAMS, n // STREAMS)] = value.astype(BF16).reshape(n // STREAMS, part_rows, width)
        if s == 0:
            trace2, loss_row = carried
        come_back.start([k for k in reversed(every_k) if (home + k) % n * STREAMS // n == s])
    tr_s[...] = stack_rows([trace2], width)
    swap_tr = Swap(tr_s, tr_r, tr_sem)
    swap_tr.start()
    swap_st.wait_recv()
    far_center, far_inv = tst_r[0:1], tst_r[1:2]
    second = ((own2[...].astype(F32) - far_center) * far_inv).astype(BF16)
    own2[...] = second
    come_back.pass_on(every_k)
    ls_s[...] = jnp.zeros((8, width), F32) + loss_row
    lc = [remote(ls_s, ls_r.at[k], ls_sem.at[0, k], ls_sem.at[1, k], to) for k, to in enumerate(y_peers)]
    for cp in lc:
        go(cp)
    for s in range(STREAMS):
        value, carried = finish(0, s)
        if s == 0:
            trace1, diag_grad = carried
        value = value + own2[stream(s)].astype(F32) * diag_grad - n1f[c, home, stream(s)].astype(F32) * trace1
        g1_o[stream(s)] = (LOSS_SCALE * value * inv1).astype(BF16)
    for cp in late:
        cp.wait_send()
    for k in range(xs):
        over(k).wait_send()
    for cp in lc:
        cp.wait_recv()
    for k in range(n - 1):
        loss_row = loss_row + ls_r[k, 0:1]
    loss_o[...] = loss_row[:, 0:1]
    swap_tr.wait_recv()
    trace2 = tr_r[0:1]
    come_back.wait_recv(every_k)
    value = ti_r[...].astype(F32) + n1f[c, home].astype(F32) * diag_grad - own2[...].astype(F32) * trace2
    g2_o[...] = (LOSS_SCALE * value * far_inv).astype(BF16)
    come_back.wait_send()
    swap_tr.wait_send()


def on_device(xs, n, view_one, view_two):
    rows, width = view_one.shape
    half = n // 2
    srow = rows // STREAMS
    prow = width // xs
    sem = pltpu.SemaphoreType.DMA
    blocks = (2, n, rows, width)
    ring = (2, 2, half, STREAMS)
    loss, grad_one, grad_two = pl.pallas_call(
        functools.partial(kernel, xs, n),
        out_shape=(
            jax.ShapeDtypeStruct((1, 1), F32),
            jax.ShapeDtypeStruct((rows, width), BF16),
            jax.ShapeDtypeStruct((rows, width), BF16),
        ),
        in_specs=[pl.BlockSpec(memory_space=pltpu.HBM)] * 2,
        out_specs=[pl.BlockSpec(memory_space=pltpu.VMEM)] * 3,
        scratch_shapes=[
            pltpu.VMEM(blocks, BF16),
            pltpu.VMEM(blocks, BF16),
            pltpu.VMEM(blocks, BF16),
            pltpu.VMEM(blocks, BF16),
            pltpu.VMEM((rows, width), BF16),
            pltpu.VMEM((n, rows // n, width), BF16),
            pltpu.VMEM((n, rows // n, width), BF16),
            pltpu.VMEM((2, 2, 8, width), F32),
            pltpu.VMEM((2, 2, 8, width), F32),
            pltpu.VMEM((8, width), F32),
            pltpu.VMEM((8, width), F32),
            pltpu.VMEM((8, width), F32),
            pltpu.VMEM((8, width), F32),
            pltpu.VMEM((2, width, width), F32),
            pltpu.VMEM((xs, 2, prow + EXTRA, width), BF16),
            pltpu.VMEM((xs - 1, 2, prow + EXTRA, width), BF16),
            pltpu.VMEM((xs, 2, prow + EXTRA, width), BF16),
            pltpu.VMEM((2, width, width), BF16),
            pltpu.VMEM((width, width), BF16),
            pltpu.VMEM((xs, prow + EXTRA, width), BF16),
            pltpu.VMEM(ring + (srow + EXTRA, width), BF16),
            pltpu.VMEM(ring + (srow + EXTRA, width), BF16),
            pltpu.VMEM((n, rows // n, width), BF16),
            pltpu.VMEM((rows, width), BF16),
            pltpu.VMEM((8, width), F32),
            pltpu.VMEM((n - 1, 8, width), F32),
            sem((2,)),
            sem((4, n)),
            sem((2,)),
            sem((2,)),
            sem(ring),
            sem(ring),
            sem((2, n + 1, STREAMS)),
            sem((2, n + 1, STREAMS)),
            sem((2, xs - 1)),
            sem((2, xs - 1)),
            sem((2, xs)),
            sem(ring),
            sem(ring),
            sem((4, n)),
            sem((2, n - 1)),
        ],
        compiler_params=pltpu.CompilerParams(
            collective_id=0, has_side_effects=True, vmem_limit_bytes=60 * 2**20
        ),
        name="barlow",
    )(view_one, view_two)
    return loss.reshape(()), grad_one, grad_two


def solution(mesh):
    n = mesh.shape["feat"] // 2
    xs = mesh.shape["batch"] // n
    spec = P("batch", "feat")
    return jax.shard_map(
        functools.partial(on_device, xs, n),
        mesh=mesh,
        in_specs=(spec, spec),
        out_specs=(P(), spec, spec),
        check_vma=False,
    )
```

```python
import functools

import jax
import jax.numpy as jnp
from jax import lax
from jax.experimental import pallas as pl
from jax.experimental.pallas import tpu as pltpu
from jax.sharding import PartitionSpec as P

OFF_WEIGHT = 0.0051
EPSILON = 1e-05
LOSS_SCALE = 16.0
MESH = pl.DeviceIdType.MESH
F32 = jnp.float32
BF16 = jnp.bfloat16
STREAMS = 2
EXTRA = 16


def split_rows(values, width):
    row_ids = lax.broadcasted_iota(jnp.int32, (EXTRA, width), 0)
    block = jnp.zeros((EXTRA, width), F32)
    for k, value in enumerate(values):
        rest = value
        for part in range(3):
            piece = rest.astype(BF16).astype(F32)
            rest = rest - piece
            block = jnp.where(row_ids == 3 * k + part, piece, block)
    return block.astype(BF16)


def join_rows(block, count):
    wide = block.astype(F32)
    return [wide[3 * k : 3 * k + 1] + wide[3 * k + 1 : 3 * k + 2] + wide[3 * k + 2 : 3 * k + 3] for k in range(count)]


def stack_rows(values, width):
    row_ids = lax.broadcasted_iota(jnp.int32, (8, width), 0)
    block = jnp.zeros((8, width), F32)
    for k, value in enumerate(values):
        block = jnp.where(row_ids == k, value, block)
    return block


def kernel(
    xs, n, v1, v2, loss_o, g1_o, g2_o,
    raw1, raw2, n1f, n2f, own2, hop_a, hop_b, ssum, qsum, tst_s, tst_r, tr_s, tr_r,
    acc, pst, pr, gx, gfull, gother, sib_r,
    rs_s, rs_r, ti_s, ti_r, ls_s, ls_r,
    in_sem, t_sem, tst_sem, tr_sem, ag_ss, ag_rs, sb_ss, sb_rs,
    px_sem, gx_sem, sib_sem, rs_ss, rs_rs, ti_sem, ls_sem,
):
    rows, width = v1.shape
    half = n // 2
    srow = rows // STREAMS
    prow = width // xs
    part_rows = rows // n
    home = n // 4
    group_rows = float(rows * n)
    total_rows = float(rows * n * xs)
    b, f = lax.axis_index("batch"), lax.axis_index("feat")
    x, y = lax.div(b, n), lax.rem(b, n)
    z, c = lax.div(f, 2), lax.rem(f, 2)
    o = 1 - c
    is_low = c == 0
    skip = half == 4

    def dev(x_, y_, z_, c_):
        return (x_ * n + y_, z_ * 2 + c_)

    def wrap(v, m):
        return lax.rem(v + m, m)

    sibling = dev(x, y, z, o)
    partner = dev(x, z, y, c)
    x_peers = [dev(wrap(x + k, xs), y, z, c) for k in range(1, xs)]
    y_peers = [dev(x, wrap(y + k, n), z, c) for k in range(1, n)]
    z_peers = [dev(x, y, wrap(z + k, n), c) for k in range(1, n)]
    nearest = sorted(range(1, n), key=lambda k: min(k, n - k))

    def along(a, k):
        return dev(x, wrap(y + k, n), z, c) if a == 0 else dev(x, y, wrap(z + k, n), c)

    ring = [[along(a, 1), along(a, -1)] for a in range(2)]
    ring2 = [[along(a, 2), along(a, -2)] for a in range(2)] if skip else None
    pos = [y, z]
    off_diag = y != z
    on_diag = y == z
    diag_one = jnp.where(on_diag, 1.0, 0.0).astype(F32)

    def remote(src, dst, ss, rs, to):
        return pltpu.make_async_remote_copy(
            src_ref=src, dst_ref=dst, send_sem=ss, recv_sem=rs, device_id=to, device_id_type=MESH
        )

    def stream(s):
        return pl.ds(s * srow, srow)

    load1 = pltpu.make_async_copy(v1, raw1.at[c, home], in_sem.at[0])
    load2 = pltpu.make_async_copy(v2, own2, in_sem.at[1])
    load1.start()
    load2.start()
    barrier = pltpu.get_barrier_semaphore()
    greet = [sibling] + x_peers + y_peers + z_peers
    for peer in greet:
        pl.semaphore_signal(barrier, inc=1, device_id=peer, device_id_type=MESH)

    @pl.when(off_diag)
    def _():
        pl.semaphore_signal(barrier, inc=1, device_id=partner, device_id_type=MESH)

    load1.wait()
    load2.wait()

    @pl.when(off_diag)
    def _():
        pl.semaphore_wait(barrier, len(greet) + 1)

    @pl.when(on_diag)
    def _():
        pl.semaphore_wait(barrier, len(greet))

    class Swap:
        def __init__(self, src, dst, sems):
            self.far = remote(src, dst, sems.at[0], sems.at[1], partner)
            self.near = pltpu.make_async_copy(src, dst, sems.at[1])

        def start(self):
            @pl.when(off_diag)
            def _():
                self.far.start()

            @pl.when(on_diag)
            def _():
                self.near.start()

        def wait_recv(self):
            @pl.when(off_diag)
            def _():
                self.far.wait_recv()

            @pl.when(on_diag)
            def _():
                self.near.wait()

        def wait_send(self):
            @pl.when(off_diag)
            def _():
                self.far.wait_send()

    late = []

    def go(cp):
        cp.start()
        late.append(cp)

    def part(k):
        return pl.ds(pl.multiple_of(k * part_rows, part_rows), part_rows)

    class Exchange:
        def __init__(self, source, hop, target, sems, along_z):
            self.source, self.hop, self.target, self.sems = source, hop, target, sems
            self.peers = z_peers if along_z else y_peers
            self.here, self.there = (z, y) if along_z else (y, z)
            self.to = (lambda k: dev(x, k, z, c)) if along_z else (lambda k: dev(x, y, k, c))

        def first(self, k):
            return remote(
                self.source(k), self.hop.at[self.here], self.sems.at[0, k], self.sems.at[1, k], self.peers[k - 1]
            )

        def stay(self):
            return pltpu.make_async_copy(self.source(0), self.hop.at[self.here], self.sems.at[1, 0])

        def second(self, k):
            origin = wrap(self.here - k, n)
            src, sem = self.hop.at[origin], self.sems.at[3, self.there]
            far = remote(src, self.target(wrap(self.there - origin, n), origin), self.sems.at[2, k], sem, self.to(origin))
            near = pltpu.make_async_copy(src, self.target(0, self.there), sem)
            return origin, far, near

        def start(self, some):
            for k in some:
                if k == 0:
                    self.stay().start()
                else:
                    self.first(k).start()

        def pass_on(self, some):
            for k in some:
                if k == 0:
                    self.stay().wait()
                else:
                    self.first(k).wait_recv()
                origin, far, near = self.second(k)

                @pl.when(origin != self.there)
                def _():
                    far.start()

                @pl.when(origin == self.there)
                def _():
                    near.start()

        def wait_recv(self, some):
            for k in some:
                ref, sem = self.target(k, self.there), self.sems.at[3, wrap(self.there + k, n)]
                if k == 0:
                    pltpu.make_async_copy(ref, ref, sem).wait()
                else:
                    remote(ref, ref, self.sems.at[2, k], sem, self.peers[0]).wait_recv()

        def wait_send(self):
            for k in nearest:
                self.first(k).wait_send()
            for k in range(n):
                origin, far, _ = self.second(k)

                @pl.when(origin != self.there)
                def _():
                    far.wait_send()

    every_k = [0] + nearest
    spread_out = Exchange(
        lambda k: own2.at[part(wrap(z + k, n))], hop_a, lambda k, _: raw2.at[c, wrap(home + k, n), part(z)], t_sem, True
    )
    spread_out.start(every_k[::-1])

    raws, norms = (raw1, raw2), (n1f, n2f)

    def depth(d, s):
        return half if (s < STREAMS // 2) == (d == 0) else half - 1

    def ring_block(a, d, t):
        if a == 0:
            return (home + (t if d else -t)) % n
        return wrap(pos[a] - t, n) if d == 0 else wrap(pos[a] + t, n)

    def piece(a, core, block, s):
        if a == 0:
            return raw1.at[core, block, stream(s)]
        return raw2.at[core, pl.ds(s * n // STREAMS, n // STREAMS), part(block)]

    def block_of(refs, a, core, block):
        if a == 0:
            return refs[core, block]
        return refs[core, :, part(block)].reshape(rows, width)

    def ag_copy(a, d, t, s):
        far = skip and t == 3
        steps = 2 if far else t
        src = piece(a, c, ring_block(a, d, steps), s)
        dst = piece(a, c, ring_block(a, d, steps + (2 if far else 1)), s) if a == 0 else src
        return remote(src, dst, ag_ss.at[a, d, t, s], ag_rs.at[a, d, t, s], (ring2 if far else ring)[a][d])

    def sib_copy(a, core, block, s, slot):
        ref = piece(a, core, block, s)
        return remote(ref, ref, sb_ss.at[a, slot, s], sb_rs.at[a, slot, s], sibling)

    def ring_slot(d, t):
        return 1 + t if d == 0 else 1 + half + t

    def open_ring(a, s):
        for d in range(2):
            if depth(d, s) > 0:
                go(ag_copy(a, d, 0, s))
        go(sib_copy(a, c, ring_block(a, 0, 0), s, 0))

    def forward(a, t):
        for s in range(STREAMS):
            for d in range(2):
                if t >= depth(d, s):
                    continue
                ag_copy(a, d, t, s).wait_recv()
                if t + 1 < min(depth(d, s), 3 if skip else half):
                    go(ag_copy(a, d, t + 1, s))
                if skip and t == 1 and depth(d, s) == 4:
                    go(ag_copy(a, d, 3, s))
                go(sib_copy(a, c, ring_block(a, d, t + 1), s, ring_slot(d, t)))

    def sib_wait(a, s, d, t):
        if d is None:
            sib_copy(a, o, ring_block(a, 0, 0), s, 0).wait_recv()
        elif t < depth(d, s):
            sib_copy(a, o, ring_block(a, d, t + 1), s, ring_slot(d, t)).wait_recv()

    shifts = {}

    def fold(value):
        return jnp.sum(value.reshape(rows // 8, 8, width), axis=0)

    def shifted(a, block, begin):
        for h, core in enumerate((c, o)):
            value = block_of(raws[a], a, core, block).astype(F32)
            if begin:
                shifts[a, h] = jnp.sum(fold(value), axis=0, keepdims=True) / rows
            value = value - shifts[a, h]
            if a == 0:
                norms[a][core, block] = value.astype(BF16)
            else:
                norms[a][core, :, part(block)] = value.astype(BF16).reshape(n, part_rows, width)
            if begin:
                ssum[a, h] = fold(value)
                qsum[a, h] = fold(value * value)
            else:
                ssum[a, h] += fold(value)
                qsum[a, h] += fold(value * value)

    def correlate(block, begin):
        for h in range(2):
            share = lax.dot_general(
                block_of(n1f, 1, c, block), block_of(n2f, 1, h, block), (((0,), (0,)), ((), ())), preferred_element_type=F32
            )
            if begin:
                acc[h] = share
            else:
                acc[h] += share

    def blocks_of(a, t):
        if t + 1 < half:
            return [ring_block(a, 0, t + 1), ring_block(a, 1, t + 1)]
        return [ring_block(a, 0, half)]

    def arrived(a, t):
        for s in range(STREAMS):
            for d in range(2):
                sib_wait(a, s, d, t)
        for block in blocks_of(a, t):
            shifted(a, block, False)

    def correlate_all(t):
        for block in blocks_of(1, t):
            correlate(block, False)

    for s in range(STREAMS):
        open_ring(0, s)
    spread_out.pass_on(every_k)
    for s in range(STREAMS):
        spread_out.wait_recv([k for k in every_k if (home + k) % n * STREAMS // n == s])
        open_ring(1, s)
    forward(0, 0)
    for s in range(STREAMS):
        sib_wait(0, s, None, 0)
    for s in range(STREAMS):
        sib_wait(1, s, None, 0)
    shifted(0, home, True)
    shifted(1, z, True)
    for t in range(1, half):
        forward(1, t - 1)
        forward(0, t)
        arrived(0, t - 1)
        if t > 1:
            arrived(1, t - 2)
    arrived(0, half - 1)
    correlate(z, True)
    for t in range(half - 2):
        correlate_all(t)
    forward(1, half - 1)
    for t in range(max(half - 2, 0), half):
        arrived(1, t)
        correlate_all(t)

    def spread(row, count, first):
        ids = lax.broadcasted_iota(jnp.int32, (count, width), 0) + first
        lanes = lax.broadcasted_iota(jnp.int32, (count, width), 1)
        return jnp.sum(jnp.where(ids == lanes, row, 0.0), axis=1, keepdims=True)

    rests, means, squares = {}, {}, {}
    for a in range(2):
        for h in range(2):
            rest = jnp.sum(ssum[a, h], axis=0, keepdims=True) / group_rows
            rests[a, h] = rest
            means[a, h] = shifts[a, h] + rest
            squares[a, h] = jnp.sum(qsum[a, h], axis=0, keepdims=True) - group_rows * rest * rest

    def by_half(table, a):
        return [jnp.where(is_low, table[a, 0], table[a, 1]), jnp.where(is_low, table[a, 1], table[a, 0])]

    rest2, mean2, square2 = by_half(rests, 1), by_half(means, 1), by_half(squares, 1)
    column = spread(rests[0, 0], width, 0) * (group_rows / total_rows)
    row_ids = lax.broadcasted_iota(jnp.int32, (width, width), 0)
    col_ids = lax.broadcasted_iota(jnp.int32, (width, width), 1)
    for h in range(2):
        acc[h] = acc[h] / total_rows - column * rest2[h]
    diag = jnp.sum(jnp.where(row_ids == col_ids, acc[c], 0.0), axis=0, keepdims=True) * diag_one
    facts = [
        [means[0, 0], squares[0, 0], mean2[0], square2[0], diag],
        [means[0, 1], squares[0, 1], mean2[1], square2[1]],
    ]

    for h in range(2):
        extra = split_rows(facts[h], width)
        for k in range(xs):
            pst[k, h, :prow] = acc[h, k * prow : (k + 1) * prow].astype(BF16)
            pst[k, h, prow:] = extra
    px = [
        remote(pst.at[wrap(x + k, xs)], pr.at[k - 1], px_sem.at[0, k - 1], px_sem.at[1, k - 1], x_peers[k - 1])
        for k in range(1, xs)
    ]
    for cp in px[1:2] + px[:1] + px[2:]:
        go(cp)
    for cp in px:
        cp.wait_recv()
    every = [facts]
    for k in range(xs - 1):
        every.append([join_rows(pr[k, 0, prow:], 5), join_rows(pr[k, 1, prow:], 4)])

    def whole(h, place):
        center = sum(e[h][place] for e in every) / xs
        spreads = [e[h][place] - center for e in every]
        square = sum(e[h][place + 1] for e in every) + group_rows * sum(v * v for v in spreads)
        return center, 1.0 / jnp.sqrt(square / total_rows + EPSILON), spreads

    center1, inv1, spread1 = whole(0, 0)
    center1o, inv1o, _ = whole(1, 0)
    center2, inv2, spread2 = [[v[h] for h in range(2)] for v in zip(*[whole(h, 2) for h in range(2)])]
    near2 = [jnp.where(is_low, v[0], v[1]) for v in (center2, inv2)]
    near_spread2 = [jnp.where(is_low, u, w) for u, w in zip(*spread2)]
    tst_s[...] = stack_rows(near2, width)
    swap_st = Swap(tst_s, tst_r, tst_sem)
    swap_st.start()

    diag = sum(e[0][4] for e in every) + sum(u * w for u, w in zip(spread1, near_spread2)) / xs * diag_one
    diag = diag * inv1 * near2[1]
    diag_grad = (-2.0 * (1.0 - diag)).astype(BF16).astype(F32) * diag_one
    prow_ids = lax.broadcasted_iota(jnp.int32, (prow, width), 0) + x * prow
    pcol_ids = lax.broadcasted_iota(jnp.int32, (prow, width), 1)
    same = prow_ids == pcol_ids
    inv_column = spread(inv1, prow, x * prow)
    spread_columns = [spread(v, prow, x * prow) / xs for v in spread1]
    loss = jnp.zeros((1, 1), F32)
    row_trace = jnp.zeros((prow, 1), F32)
    col_trace = []
    for h in range(2):
        corr = acc[h, pl.ds(pl.multiple_of(x * prow, prow), prow)]
        for k in range(xs - 1):
            corr = corr + pr[k, h, :prow].astype(F32)
        for k in range(xs):
            corr = corr + spread_columns[k] * spread2[h][k]
        corr = corr * inv_column * inv2[h]
        spot = same & on_diag & (c == h)
        terms = jnp.where(spot, (1.0 - diag) * (1.0 - diag), OFF_WEIGHT * corr * corr)
        loss = loss + jnp.sum(jnp.sum(terms, axis=0, keepdims=True), axis=1, keepdims=True)
        grad = jnp.where(spot, 0.0, 2.0 * OFF_WEIGHT * corr).astype(BF16)
        gx[x, h, :prow] = grad
        share = corr * grad.astype(F32)
        row_trace = row_trace + jnp.sum(share, axis=1, keepdims=True)
        col_trace.append(jnp.sum(share, axis=0, keepdims=True))
    row_trace = jnp.sum(jnp.where(same, row_trace, 0.0), axis=0, keepdims=True)
    loss_row = jnp.zeros((1, width), F32) + loss
    gx[x, 0, prow:] = split_rows([col_trace[0], row_trace, loss_row], width)
    gx[x, 1, prow:] = split_rows([col_trace[1], row_trace, loss_row], width)
    gc = [remote(gx.at[x], gx.at[x], gx_sem.at[0, k], gx_sem.at[1, k], to) for k, to in enumerate(x_peers)]
    for cp in gc[1:2] + gc[:1] + gc[2:]:
        cp.start()

    def over(k):
        return remote(gx.at[k, o], sib_r.at[k], sib_sem.at[0, k], sib_sem.at[1, k], sibling)

    over(x).start()

    def standard(i, _):
        n1f[c, i] = ((raw1[c, i].astype(F32) - center1) * inv1).astype(BF16)
        n1f[o, i] = ((raw1[o, i].astype(F32) - center1o) * inv1o).astype(BF16)
        for h in range(2):
            n2f[h, i] = ((raw2[h, i].astype(F32) - center2[h]) * inv2[h]).astype(BF16)
        return 0

    lax.fori_loop(0, n, standard, 0)
    for cp in late:
        cp.wait_send()
    spread_out.wait_send()
    swap_st.wait_send()
    for k in range(1, xs):
        src = wrap(x - k, xs)
        remote(gx.at[src], gx.at[src], gx_sem.at[0, k - 1], gx_sem.at[1, k - 1], x_peers[k - 1]).wait_recv()
        over(src).start()
    col0 = col1 = trace1 = loss_row = jnp.zeros((1, width), F32)
    for k in range(xs):
        for h in range(2):
            gfull[h, k * prow : (k + 1) * prow] = gx[k, h, :prow]
        got = join_rows(gx[k, 0, prow:], 3)
        col0, trace1, loss_row = col0 + got[0], trace1 + got[1], loss_row + got[2]
        col1 = col1 + join_rows(gx[k, 1, prow:], 1)[0]
    diag_trace = diag * diag_grad
    trace1 = trace1 + diag_trace
    trace2 = jnp.where(is_low, col0, col1) + diag_trace
    late = gc
    for k in range(xs):
        over(k).wait_recv()
    for k in range(xs):
        gother[k * prow : (k + 1) * prow] = sib_r[k, :prow]
        got = join_rows(sib_r[k, prow:], 3)
        trace2 = trace2 + got[0]
        loss_row = loss_row + got[2]

    ring_extra = [[trace1, diag_grad], [trace2, loss_row]]

    def product(a, block, s):
        if a == 0:
            dims = (((1,), (1,)), ((), ()))
            left, right = [n2f[h, block, stream(s)] for h in range(2)], (gfull[0], gfull[1])
        else:
            dims = (((1,), (0,)), ((), ()))
            images = pl.ds(s * n // STREAMS, n // STREAMS)
            left = [n1f[h, images, part(block)].reshape(srow, width) for h in (c, o)]
            right = (gfull[c], gother[...])
        return lax.dot_general(left[0], right[0], dims, preferred_element_type=F32) + lax.dot_general(
            left[1], right[1], dims, preferred_element_type=F32
        )

    def rs_copy(a, d, t, s):
        far = skip and t == 0 and depth(d, s) == 4
        sub = pl.ds(0, srow + (EXTRA if s == 0 else 0))
        return remote(
            rs_s.at[a, d, t, s, sub], rs_r.at[a, d, t, s, sub], rs_ss.at[a, d, t, s], rs_rs.at[a, d, t, s],
            (ring2 if far else ring)[a][d],
        )

    def takes(d, t, s):
        if skip and depth(d, s) == 4:
            return {0: [], 1: [], 2: [0, 1], 3: [2]}[t]
        return [t - 1] if t > 0 else []

    def add_in(a, d, s, value, carried, messages):
        for m in messages:
            rs_copy(a, d, m, s).wait_recv()
            value = value + rs_r[a, d, m, s, :srow].astype(F32)
            if s == 0:
                got = join_rows(rs_r[a, d, m, s, srow:], 2)
                carried = [u + w for u, w in zip(carried, got)]
        return value, carried

    def rs_send(a, d, t, s):
        block = ring_block(a, 1 - d, depth(d, s) - t)
        value, carried = add_in(a, d, s, product(a, block, s), ring_extra[a], takes(d, t, s))
        rs_s[a, d, t, s, :srow] = value.astype(BF16)
        if s == 0:
            rs_s[a, d, t, s, srow:] = split_rows(carried, width)
        go(rs_copy(a, d, t, s))

    lanes = [(s, a, d) for s in reversed(range(STREAMS)) for a in (1, 0) for d in range(2)]
    for step in range(half):
        for s, a, d in lanes:
            deep = depth(d, s)
            if skip and deep == 4:
                for t in ([0, 1], [2], [3], [])[step]:
                    rs_send(a, d, t, s)
            elif step < deep:
                rs_send(a, d, step, s)

    def finish(a, s):
        value, carried = product(a, ring_block(a, 0, 0), s), ring_extra[a]
        for d in range(2):
            if depth(d, s) > 0:
                value, carried = add_in(a, d, s, value, carried, [depth(d, s) - 1])
        return value, carried

    come_back = Exchange(
        lambda k: ti_s.at[(home + k) % n], hop_b, lambda k, base: ti_r.at[part(wrap(base + k, n))], ti_sem, False
    )
    for s in reversed(range(STREAMS)):
        value, carried = finish(1, s)
        ti_s[pl.ds(s * n // STREAMS, n // STREAMS)] = value.astype(BF16).reshape(n // STREAMS, part_rows, width)
        if s == 0:
            trace2, loss_row = carried
        come_back.start([k for k in reversed(every_k) if (home + k) % n * STREAMS // n == s])
    tr_s[...] = stack_rows([trace2], width)
    swap_tr = Swap(tr_s, tr_r, tr_sem)
    swap_tr.start()
    swap_st.wait_recv()
    far_center, far_inv = tst_r[0:1], tst_r[1:2]
    second = ((own2[...].astype(F32) - far_center) * far_inv).astype(BF16)
    own2[...] = second
    for s in range(STREAMS):
        value, carried = finish(0, s)
        if s == 0:
            trace1, diag_grad = carried
        value = value + own2[stream(s)].astype(F32) * diag_grad - n1f[c, home, stream(s)].astype(F32) * trace1
        g1_o[stream(s)] = (LOSS_SCALE * value * inv1).astype(BF16)
    come_back.pass_on(every_k)
    ls_s[...] = jnp.zeros((8, width), F32) + loss_row
    lc = [remote(ls_s, ls_r.at[k], ls_sem.at[0, k], ls_sem.at[1, k], to) for k, to in enumerate(y_peers)]
    for cp in lc:
        go(cp)
    for cp in late:
        cp.wait_send()
    for k in range(xs):
        over(k).wait_send()
    for cp in lc:
        cp.wait_recv()
    for k in range(n - 1):
        loss_row = loss_row + ls_r[k, 0:1]
    loss_o[...] = loss_row[:, 0:1]
    swap_tr.wait_recv()
    trace2 = tr_r[0:1]
    come_back.wait_recv(every_k)
    value = ti_r[...].astype(F32) + n1f[c, home].astype(F32) * diag_grad - own2[...].astype(F32) * trace2
    g2_o[...] = (LOSS_SCALE * value * far_inv).astype(BF16)
    come_back.wait_send()
    swap_tr.wait_send()


def on_device(xs, n, view_one, view_two):
    rows, width = view_one.shape
    half = n // 2
    srow = rows // STREAMS
    prow = width // xs
    sem = pltpu.SemaphoreType.DMA
    blocks = (2, n, rows, width)
    ring = (2, 2, half, STREAMS)
    loss, grad_one, grad_two = pl.pallas_call(
        functools.partial(kernel, xs, n),
        out_shape=(
            jax.ShapeDtypeStruct((1, 1), F32),
            jax.ShapeDtypeStruct((rows, width), BF16),
            jax.ShapeDtypeStruct((rows, width), BF16),
        ),
        in_specs=[pl.BlockSpec(memory_space=pltpu.HBM)] * 2,
        out_specs=[pl.BlockSpec(memory_space=pltpu.VMEM)] * 3,
        scratch_shapes=[
            pltpu.VMEM(blocks, BF16),
            pltpu.VMEM(blocks, BF16),
            pltpu.VMEM(blocks, BF16),
            pltpu.VMEM(blocks, BF16),
            pltpu.VMEM((rows, width), BF16),
            pltpu.VMEM((n, rows // n, width), BF16),
            pltpu.VMEM((n, rows // n, width), BF16),
            pltpu.VMEM((2, 2, 8, width), F32),
            pltpu.VMEM((2, 2, 8, width), F32),
            pltpu.VMEM((8, width), F32),
            pltpu.VMEM((8, width), F32),
            pltpu.VMEM((8, width), F32),
            pltpu.VMEM((8, width), F32),
            pltpu.VMEM((2, width, width), F32),
            pltpu.VMEM((xs, 2, prow + EXTRA, width), BF16),
            pltpu.VMEM((xs - 1, 2, prow + EXTRA, width), BF16),
            pltpu.VMEM((xs, 2, prow + EXTRA, width), BF16),
            pltpu.VMEM((2, width, width), BF16),
            pltpu.VMEM((width, width), BF16),
            pltpu.VMEM((xs, prow + EXTRA, width), BF16),
            pltpu.VMEM(ring + (srow + EXTRA, width), BF16),
            pltpu.VMEM(ring + (srow + EXTRA, width), BF16),
            pltpu.VMEM((n, rows // n, width), BF16),
            pltpu.VMEM((rows, width), BF16),
            pltpu.VMEM((8, width), F32),
            pltpu.VMEM((n - 1, 8, width), F32),
            sem((2,)),
            sem((4, n)),
            sem((2,)),
            sem((2,)),
            sem(ring),
            sem(ring),
            sem((2, n + 1, STREAMS)),
            sem((2, n + 1, STREAMS)),
            sem((2, xs - 1)),
            sem((2, xs - 1)),
            sem((2, xs)),
            sem(ring),
            sem(ring),
            sem((4, n)),
            sem((2, n - 1)),
        ],
        compiler_params=pltpu.CompilerParams(
            collective_id=0, has_side_effects=True, vmem_limit_bytes=60 * 2**20
        ),
        name="barlow",
    )(view_one, view_two)
    return loss.reshape(()), grad_one, grad_two


def solution(mesh):
    n = mesh.shape["feat"] // 2
    xs = mesh.shape["batch"] // n
    spec = P("batch", "feat")
    return jax.shard_map(
        functools.partial(on_device, xs, n),
        mesh=mesh,
        in_specs=(spec, spec),
        out_specs=(P(), spec, spec),
        check_vma=False,
    )
```
